128 devices in a mesh: lat: 32 (over y, x, core), swath: 4 (over z).
Axes of the slice: x: 4, y: 4, z: 4, core: 2. Of those that a mesh axis runs over, the one named last changes fastest.
Arguments:
- saved_state: float32 [6, 16, 512, 1024], P(None, None, 'lat', 'swath'), may hold values from 0.35 to 0.45
- background_increment: float32 [16, 512, 1024], P(None, 'lat', 'swath'), may hold values from -2.5 to 2.5
- obs_residual: float32 [128, 128, 6, 128], P(('lat', 'swath')), may hold values from -6 to 6
- obs_weight: float32 [128, 128, 6, 128], P(('lat', 'swath')), may hold values from 0.3 to 3
- obs_kernel: float32 [128, 128, 6, 4, 128], P(('lat', 'swath')), may hold values from 0.1 to 1
- obs_cell: int32 [128, 128, 6, 128], P(('lat', 'swath')), may hold values from 0 to 1023
- obs_count: int32 [128, 128, 6], P(('lat', 'swath')), may hold values from 0 to 128, as said below
Outputs:
- gradient: float32 [16, 512, 1024], P(None, 'lat', 'swath')
The draws below stay inside these ranges and needn't reach their ends.
Inputs may be any that keep to these rules, and one draw needn't show every extreme that they name: `obs_count`: slots at or beyond the count are padding. In every step one tile receives 128 footprints from every owner.
All inputs are finite; a program needn't handle non-finite values.
Results may differ from the reference program's by a relative error of at most 0.00011.
Values sent between devices are 32-bit elements; how exact they have to be, the bound alone decides.
A program may use at most 128 MiB of HBM per device.

```python
import math
import jax
import jax.numpy as jnp

CX = 16
CY = 256
NZ = 16
STEPS = 6
CAP = 128
FOOT = 4
TILES = 128
NX = 512
NY = 1024
N_SWATH = 4


def draw_obs_count(key, part):
    base_key, hot_key = jax.random.split(jax.random.fold_in(key, 17))
    base_count = jax.random.randint(base_key, (TILES, TILES, STEPS), 0, 3 * CAP // 4 + 1)
    hottest = jax.random.randint(hot_key, (STEPS,), 0, TILES)
    target = jnp.arange(TILES, dtype=jnp.int32)[None, :, None]
    return jnp.where(target == hottest[None, None, :], CAP, base_count).astype(jnp.int32)


def with_ends(entries, rng, smallest, largest):
    place = [jax.random.randint(jax.random.fold_in(rng, axis), (), 0, length) for axis, length in enumerate(entries.shape)]
    widest = entries.shape.index(max(entries.shape))
    beside = place[:widest] + [(place[widest] + 1) % entries.shape[widest]] + place[widest + 1:]
    return entries.at[tuple(place)].set(smallest).at[tuple(beside)].set(largest)


def block_levels(stream_key, shape, cuts, smallest, high):
    def one(axis_at, blocks):
        draws = jax.random.uniform(jax.random.fold_in(jax.random.fold_in(stream_key, 6), axis_at), (blocks,), jnp.float32, smallest / len(cuts), high / len(cuts))
        return jnp.repeat(jnp.exp(draws), shape[axis_at] // blocks).reshape((-1,) + (1,) * (len(shape) - axis_at - 1))

    factor_of = one(*cuts[0])
    for cut in cuts[1:]:
        factor_of = factor_of * one(*cut)
    return factor_of


def scatter_about(rng, shape, scale, most, cuts=(), held_as=jnp.bfloat16):
    entries = scale * jax.random.normal(rng, shape, jnp.float32)
    if cuts:
        entries = entries * block_levels(rng, shape, cuts, -0.22, 0.18)
    return jnp.clip(entries, -most, most).astype(held_as)


def setup_inputs(seed: int = 0) -> dict:
    streams_of = jax.random.split(jax.random.key(seed), 8)
    saved_state = jnp.clip(0.35 + 0.099999994 * jax.random.uniform(streams_of[0], (STEPS, NZ, NX, NY), jnp.float32) ** block_levels(streams_of[0], (STEPS, NZ, NX, NY), ((2, 32), (3, 4)), -0.2, 0.2), 0.35, 0.45)
    background_increment = scatter_about(streams_of[1], (NZ, NX, NY), 0.2, 2.5, ((1, 32), (2, 4)), jnp.float32)
    obs_residual = scatter_about(streams_of[2], (TILES, TILES, STEPS, CAP), 1.0, 6.0, ((0, 128),), jnp.float32)
    obs_weight = jnp.clip(jnp.exp(math.log(3.0) - 2.3025851 * jax.random.uniform(streams_of[3], (TILES, TILES, STEPS, CAP), jnp.float32) ** block_levels(streams_of[3], (TILES, TILES, STEPS, CAP), ((0, 128),), -0.2, 0.2)), 0.3, 3.0)
    obs_kernel = jnp.clip(0.1 + 0.9 * jax.random.uniform(streams_of[4], (TILES, TILES, STEPS, FOOT, CAP), jnp.float32) ** block_levels(streams_of[4], (TILES, TILES, STEPS, FOOT, CAP), ((0, 128),), -0.2, 0.2), 0.1, 1.0)
    obs_cell = with_ends(jax.random.randint(streams_of[5], (TILES, TILES, STEPS, CAP), 0, CX * CY // FOOT), jax.random.fold_in(streams_of[5], 1), 0, (CX * CY // FOOT) - 1).astype(jnp.int32)
    obs_count = draw_obs_count(jax.random.fold_in(streams_of[7], 71), 0)
    return dict(saved_state=saved_state, background_increment=background_increment, obs_residual=obs_residual, obs_weight=obs_weight, obs_kernel=obs_kernel, obs_cell=obs_cell, obs_count=obs_count)


SAT = 0.45
LATERAL = 0.1
VERTICAL = 0.25
DRAIN = 0.03


def transposed_step(field_pad, state_pad):
    relative = state_pad / SAT
    conduct_pad = relative * relative * relative
    field = field_pad[:, 1:-1, 1:-1]
    conduct = conduct_pad[:, 1:-1, 1:-1]
    drainage = 3.0 * relative[:, 1:-1, 1:-1] * relative[:, 1:-1, 1:-1]
    lateral = jnp.zeros_like(field)
    pairs = ((field_pad[:, 2:, 1:-1], conduct_pad[:, 2:, 1:-1]),
             (field_pad[:, :-2, 1:-1], conduct_pad[:, :-2, 1:-1]),
             (field_pad[:, 1:-1, 2:], conduct_pad[:, 1:-1, 2:]),
             (field_pad[:, 1:-1, :-2], conduct_pad[:, 1:-1, :-2]))
    for neighbour, cond_nb in pairs:
        lateral = lateral + 0.5 * (conduct + cond_nb) * (neighbour - field)
    interface = 0.5 * (conduct[1:] + conduct[:-1]) * (field[1:] - field[:-1])
    zero_layer = jnp.zeros_like(field[:1])
    vertical = jnp.concatenate([interface, zero_layer], 0) - jnp.concatenate([zero_layer, interface], 0)
    beneath = jnp.concatenate([field[1:], zero_layer], 0)
    return field + LATERAL * lateral + VERTICAL * vertical + DRAIN * drainage * (beneath - field)


def background_term(field_pad):
    field = field_pad[:, 1:-1, 1:-1]
    beside_all = field_pad[:, 2:, 1:-1] + field_pad[:, :-2, 1:-1] + field_pad[:, 1:-1, 2:] + field_pad[:, 1:-1, :-2]
    return 0.5 * (field + 0.2 * (4.0 * field - beside_all))


def forcing(obs_residual, obs_weight, obs_kernel, obs_cell, obs_count, step):
    tiles = obs_count.shape[0]
    slots = obs_residual.shape[-1]
    occupied = jnp.arange(slots, dtype=jnp.int32)[None, None, :] < obs_count[:, :, step][:, :, None]
    scaled = jnp.where(occupied, obs_weight[:, :, step] * obs_residual[:, :, step], 0.0)
    target = jnp.arange(tiles, dtype=jnp.int32)[None, :, None]
    quarter = CY // FOOT
    anchor = obs_cell[:, :, step]
    grid_row = (target // N_SWATH) * CX + anchor // quarter
    grid_col = (target % N_SWATH) * CY + (anchor % quarter) * FOOT
    surface = jnp.zeros((NX * NY,), jnp.float32)
    for offset in range(FOOT):
        contrib = scaled * obs_kernel[:, :, step, offset]
        where_to = (grid_row * NY + grid_col + offset).astype(jnp.int32)
        surface = surface + jax.ops.segment_sum(contrib.ravel(), where_to.ravel(), num_segments=NX * NY)
    return surface.reshape(NX, NY)


def reference(saved_state, background_increment, obs_residual, obs_weight, obs_kernel, obs_cell, obs_count):
    widths = ((0, 0), (1, 1), (1, 1))
    adjoint = jnp.zeros(saved_state.shape[1:], jnp.float32)
    for step in range(STEPS - 1, -1, -1):
        surface = forcing(obs_residual, obs_weight, obs_kernel, obs_cell, obs_count, step)
        adjoint = adjoint.at[0].add(surface)
        adjoint = transposed_step(jnp.pad(adjoint, widths), jnp.pad(saved_state[step], widths))
    return adjoint + background_term(jnp.pad(background_increment, widths))
```

```python
import functools

import jax
import jax.numpy as jnp
from jax import lax
from jax.experimental import pallas as pl
from jax.experimental.pallas import tpu as pltpu
from jax.sharding import PartitionSpec as P

MESH = pl.DeviceIdType.MESH
F32 = jnp.float32
BF16 = jnp.bfloat16

SAT = 0.45
STEPS = 6
NZ = 16
ROWS = 16
LANES = 128
HALVES = 2
FOOT = 4

NY4 = 4
NI = 8
NZ4 = 4
NA = NY4 * NZ4


def iota(shape, dim):
    return lax.broadcasted_iota(jnp.int32, shape, dim)


def kernel(
    sv, bg, res, wgt, cell, ker, cnt, out,
    S, R, W, C, KV, CT, sendA, recvA, sendB, recvB, SHs, SHr, HS, HR,
    CF, KK, BG, V, E, PRE,
    in_sem, st_sem, a_send, a_recv, b_send, b_recv, sh_send, sh_recv, h_send, h_recv,
):
    lat = lax.axis_index("lat")
    z = lax.axis_index("swath")
    y = lat // NI
    me_i = lat % NI
    nlat = NY4 * NI

    loads = [
        pltpu.make_async_copy(res, R, in_sem.at[0]),
        pltpu.make_async_copy(wgt, W, in_sem.at[1]),
        pltpu.make_async_copy(cell, C, in_sem.at[2]),
        pltpu.make_async_copy(ker, KV, in_sem.at[3]),
    ]
    states = []
    for h in range(HALVES):
        cols = pl.ds(h * LANES, LANES)
        states.append(
            pltpu.make_async_copy(
                sv.at[:, :, :, cols], S.at[pl.ds(0, STEPS), h], st_sem.at[h]
            )
        )
        states.append(pltpu.make_async_copy(bg.at[:, :, cols], S.at[STEPS, h], st_sem.at[2 + h]))
    for c in states:
        c.start()
    for c in loads:
        c.start()

    barrier = pltpu.get_barrier_semaphore()
    for r in range(1, NA):
        ty = (y + r // NZ4) % NY4
        tz = (z + r % NZ4) % NZ4
        pl.semaphore_signal(barrier, inc=1, device_id=(ty * NI + me_i, tz), device_id_type=MESH)
    for k in range(1, NI):
        pl.semaphore_signal(
            barrier, inc=1, device_id=(y * NI + (me_i + k) % NI, z), device_id_type=MESH
        )
    up = (lat + nlat - 1) % nlat
    down = (lat + 1) % nlat
    left = (z + NZ4 - 1) % NZ4
    right = (z + 1) % NZ4
    pl.semaphore_signal(barrier, inc=1, device_id=(up, z), device_id_type=MESH)
    pl.semaphore_signal(barrier, inc=1, device_id=(down, z), device_id_type=MESH)

    lane8 = iota((8, LANES), 1)
    lane = iota((ROWS, LANES), 1)
    row = iota((ROWS, LANES), 0)

    counts = jnp.concatenate([cnt[...].astype(F32), jnp.zeros((LANES - STEPS, LANES), F32)], 0)
    CT[...] = jnp.transpose(counts, (1, 0))

    def build(q, carry):
        rr = iota((LANES, 512), 0)
        cc = iota((LANES, 512), 1)
        hit = ((rr >> 6) == (cc >> 8)) & (((rr & 63) * FOOT + q) == (cc & 255))
        E[pl.ds(pl.multiple_of(q * LANES, LANES), LANES), :] = jnp.where(hit, 1.0, 0.0).astype(BF16)
        return carry

    lax.fori_loop(0, FOOT, build, 0)

    for c in states:
        c.wait()

    S2 = S.reshape((STEPS + 1) * HALVES * NZ * ROWS, LANES)

    def state_edges(t, carry):
        for h in range(HALVES):
            base = (t * HALVES + h) * NZ * ROWS
            SHs[t, h] = S2[pl.ds(base + ROWS - 1, NZ, stride=ROWS), :]
            SHs[t, 2 + h] = S2[pl.ds(base, NZ, stride=ROWS), :]
        p4 = jnp.zeros((ROWS, LANES), F32)
        p5 = jnp.zeros((ROWS, LANES), F32)
        for l in range(NZ):
            p4 = jnp.where(lane == l, S[t, 1, l][:, LANES - 1:], p4)
            p5 = jnp.where(lane == l, S[t, 0, l][:, :1], p5)
        SHs[t, 4] = p4
        SHs[t, 5] = p5
        return carry

    lax.fori_loop(0, STEPS + 1, state_edges, 0)

    pl.semaphore_wait(barrier, NA - 1 + NI - 1 + 2)

    routes = ((0, 2, (down, z)), (2, 2, (up, z)), (4, 1, (lat, right)), (5, 1, (lat, left)))

    def state_copies():
        return [
            pltpu.make_async_remote_copy(
                src_ref=SHs.at[:, pl.ds(first, many)],
                dst_ref=SHr.at[:, pl.ds(first, many)],
                send_sem=sh_send.at[n],
                recv_sem=sh_recv.at[n],
                device_id=to,
                device_id_type=MESH,
            )
            for n, (first, many, to) in enumerate(routes)
        ]

    for c in state_copies():
        c.start()

    for c in loads:
        c.wait()

    def weigh(t, yp, zp):
        d0 = yp * 32 + zp
        rows = pl.ds(t * LANES + d0, NI, stride=4)
        held = jnp.sum(jnp.where(lane8 == t, CT[pl.ds(d0, NI, stride=4), :], 0.0), 1, keepdims=True)
        scaled = jnp.where(lane8.astype(F32) < held, R[rows, :] * W[rows, :], 0.0)
        parts = [
            scaled * KV[pl.ds(d0 * STEPS * FOOT + t * FOOT + j, NI, stride=4 * STEPS * FOOT), :]
            for j in range(FOOT)
        ]
        return parts + [C[rows, :].astype(F32)]

    def stage_a_step(s, carry):
        t = STEPS - 1 - s

        def one(r, carry):
            ty = (y + r // NZ4) % NY4
            tz = (z + r % NZ4) % NZ4
            for q, part in enumerate(weigh(t, ty, tz)):
                sendA[t, r - 1, q] = part
            pltpu.make_async_remote_copy(
                src_ref=sendA.at[t, r - 1],
                dst_ref=recvA.at[t, r - 1],
                send_sem=a_send,
                recv_sem=a_recv.at[t],
                device_id=(ty * NI + me_i, tz),
                device_id_type=MESH,
            ).start()
            return carry

        lax.fori_loop(1, NA, one, 0)
        for q, part in enumerate(weigh(t, y, z)):
            recvA[t, NA - 1, q] = part
        return carry

    lax.fori_loop(0, STEPS, stage_a_step, 0)

    for c in state_copies():
        c.wait_recv()

    has_up = (lat > 0).astype(F32)
    has_down = (lat < nlat - 1).astype(F32)
    has_left = (z > 0).astype(F32)
    has_right = (z < NZ4 - 1).astype(F32)

    def cube(x):
        rel = x * (1.0 / SAT)
        return rel * rel * rel

    def around(halves, tops, bottoms, lefts, rights, h):
        x = halves[h]
        above = jnp.where(row == 0, tops[h], pltpu.roll(x, 1, 0))
        below = jnp.where(row == ROWS - 1, bottoms[h], pltpu.roll(x, ROWS - 1, 0))
        before = lefts if h == 0 else pltpu.roll(halves[0], 1, 1)
        before = jnp.where(lane == 0, before, pltpu.roll(x, 1, 1))
        after = rights if h == 1 else pltpu.roll(halves[1], LANES - 1, 1)
        after = jnp.where(lane == LANES - 1, after, pltpu.roll(x, LANES - 1, 1))
        return above, below, before, after

    def coefficients(s, carry):
        t = STEPS - 1 - s
        for l in range(NZ):
            for h in range(HALVES):
                KK[h, l] = cube(S[t, h, l])
        tops = [cube(SHr[t, h]) * has_up for h in range(HALVES)]
        bottoms = [cube(SHr[t, 2 + h]) * has_down for h in range(HALVES)]
        lefts = cube(SHr[t, 4]) * has_left
        rights = cube(SHr[t, 5]) * has_right
        for l in range(NZ):
            halves = [KK[0, l], KK[1, l]]
            for h in range(HALVES):
                k = halves[h]
                near = around(
                    halves,
                    [x[l:l + 1] for x in tops],
                    [x[l:l + 1] for x in bottoms],
                    lefts[:, l:l + 1],
                    rights[:, l:l + 1],
                    h,
                )
                cs = [0.05 * (k + x) for x in near]
                total = (cs[0] + cs[1]) + (cs[2] + cs[3])
                cs[0] = jnp.where(row == 0, cs[0] * has_up, cs[0])
                cs[1] = jnp.where(row == ROWS - 1, cs[1] * has_down, cs[1])
                if h == 0:
                    cs[2] = jnp.where(lane == 0, cs[2] * has_left, cs[2])
                else:
                    cs[3] = jnp.where(lane == LANES - 1, cs[3] * has_right, cs[3])
                rel = S[t, h, l] * (1.0 / SAT)
                drain = (0.03 * 3.0) * rel * rel
                total = total + drain
                for n in range(4):
                    CF[t, 1 + n, h, l] = cs[n]
                if l > 0:
                    over = 0.125 * (k + KK[h, l - 1])
                    CF[t, 5, h, l] = over
                    total = total + over
                if l < NZ - 1:
                    under = 0.125 * (k + KK[h, l + 1])
                    CF[t, 6, h, l] = under + drain
                    total = total + under
                CF[t, 0, h, l] = 1.0 - total
        return carry

    lax.fori_loop(0, STEPS, coefficients, 0)

    tops = [SHr[STEPS, h] * has_up for h in range(HALVES)]
    bottoms = [SHr[STEPS, 2 + h] * has_down for h in range(HALVES)]
    lefts = SHr[STEPS, 4] * has_left
    rights = SHr[STEPS, 5] * has_right
    for l in range(NZ):
        halves = [S[STEPS, 0, l], S[STEPS, 1, l]]
        for h in range(HALVES):
            near = around(
                halves,
                [x[l:l + 1] for x in tops],
                [x[l:l + 1] for x in bottoms],
                lefts[:, l:l + 1],
                rights[:, l:l + 1],
                h,
            )
            BG[h, l] = 0.9 * halves[h] - 0.1 * ((near[0] + near[1]) + (near[2] + near[3]))

    V[...] = jnp.zeros_like(V)

    n_iota = iota((LANES, LANES), 0).astype(F32).astype(BF16)
    a_iota = iota((8, LANES), 0).astype(F32)

    def gather(t):
        pltpu.make_async_copy(
            recvA.at[t, pl.ds(0, NA - 1)], recvA.at[t, pl.ds(0, NA - 1)], a_recv.at[t]
        ).wait()

        def split(o, carry):
            anchor = recvA[t, o, FOOT]
            r = jnp.floor(anchor * (1.0 / 64.0))
            b = jnp.floor(anchor * (1.0 / 512.0))
            PRE[o, 8] = (anchor - 64.0 * r) + 64.0 * b
            PRE[o, 9] = r - 8.0 * b
            for j in range(FOOT):
                v = recvA[t, o, j]
                hi = v.astype(BF16).astype(F32)
                PRE[o, 2 * j] = hi
                PRE[o, 2 * j + 1] = v - hi
            return carry

        lax.fori_loop(0, NA, split, 0)

        def tile(k, carry):
            i = (me_i + k) % NI
            acc = jnp.zeros((FOOT * 16, LANES), F32)
            for o in range(0, NA, 2):
                lhs, rhs = [], []
                for oo in (o, o + 1):
                    def spread(q, n):
                        return jnp.broadcast_to(PRE[oo, q, pl.ds(i, 1), :], (n, LANES))

                    here = a_iota == spread(9, 8)
                    cols = []
                    for q in range(2 * FOOT):
                        cols.append(jnp.where(here, spread(q, 8), 0.0))
                    lhs.append(jnp.concatenate(cols, 0).astype(BF16))
                    hot = n_iota == jnp.broadcast_to(spread(8, 16).astype(BF16)[:1], (LANES, LANES))
                    rhs.append(jnp.where(hot, jnp.ones((), BF16), jnp.zeros((), BF16)))
                acc = acc + lax.dot_general(
                    jnp.concatenate(lhs, 1),
                    jnp.concatenate(rhs, 1),
                    (((1,), (1,)), ((), ())),
                    preferred_element_type=F32,
                )
            sums = [acc[16 * j:16 * j + 8] + acc[16 * j + 8:16 * j + 16] for j in range(FOOT)]

            @pl.when(k < NI)
            def _():
                for j in range(FOOT):
                    sendB[t, k - 1, j] = sums[j]
                pltpu.make_async_remote_copy(
                    src_ref=sendB.at[t, k - 1],
                    dst_ref=recvB.at[t, k - 1],
                    send_sem=b_send,
                    recv_sem=b_recv.at[t],
                    device_id=(y * NI + i, z),
                    device_id_type=MESH,
                ).start()

            @pl.when(k == NI)
            def _():
                for j in range(FOOT):
                    recvB[t, NI - 1, j] = sums[j]

            return carry

        lax.fori_loop(1, NI + 1, tile, 0)

    def forcing(t):
        pltpu.make_async_copy(
            recvB.at[t, pl.ds(0, NI - 1)], recvB.at[t, pl.ds(0, NI - 1)], b_recv.at[t]
        ).wait()
        xs = []
        for j in range(FOOT):
            x = recvB[t, 0, j]
            for k in range(1, NI):
                x = x + recvB[t, k, j]
            xs.append(x)
        x = jnp.concatenate(xs, 1)
        hi = x.astype(BF16).astype(F32)
        both = jnp.concatenate([hi, x - hi], 0).astype(BF16)
        f = jnp.dot(both, E[...], preferred_element_type=F32)
        f = f[:8] + f[8:]
        return [
            jnp.concatenate(
                [f[:, h * LANES:(h + 1) * LANES], f[:, 256 + h * LANES:256 + (h + 1) * LANES]], 0
            )
            for h in range(HALVES)
        ]

    def edge_copies(t):
        return [
            pltpu.make_async_remote_copy(
                src_ref=HS.at[t, pl.ds(first, many)],
                dst_ref=HR.at[t, pl.ds(first, many)],
                send_sem=h_send,
                recv_sem=h_recv.at[t],
                device_id=to,
                device_id_type=MESH,
            )
            for first, many, to in routes
        ]

    V2 = V.reshape(HALVES * NZ * ROWS * 2, LANES)

    def send_edges(t, p4, p5):
        slot = t % 2
        for h in range(HALVES):
            base = (slot * HALVES + h) * NZ * ROWS
            HS[t, h] = V2[pl.ds(base + ROWS - 1, NZ, stride=ROWS), :]
            HS[t, 2 + h] = V2[pl.ds(base, NZ, stride=ROWS), :]
        HS[t, 4] = p4
        HS[t, 5] = p5
        for c in edge_copies(t):
            c.start()

    def stencil(t, put):
        slot = t % 2
        pltpu.make_async_copy(HR.at[t], HR.at[t], h_recv.at[t]).wait()
        lefts = HR[t, 4]
        rights = HR[t, 5]
        for l in range(NZ):
            halves = [V[slot, 0, l], V[slot, 1, l]]
            made = []
            for h in range(HALVES):
                near = around(
                    halves,
                    [HR[t, g, pl.ds(l, 1), :] for g in (0, 1)],
                    [HR[t, g, pl.ds(l, 1), :] for g in (2, 3)],
                    lefts[:, l:l + 1],
                    rights[:, l:l + 1],
                    h,
                )
                terms = [CF[t, 0, h, l] * halves[h]]
                terms += [CF[t, 1 + n, h, l] * near[n] for n in range(4)]
                if l > 0:
                    terms.append(CF[t, 5, h, l] * V[slot, h, l - 1])
                if l < NZ - 1:
                    terms.append(CF[t, 6, h, l] * V[slot, h, l + 1])
                total = terms[0]
                for term in terms[1:]:
                    total = total + term
                made.append(total)
            put(l, made)

    def first_edges():
        t = STEPS - 1
        f = forcing(t)
        p4 = jnp.where(lane == 0, f[1][:, LANES - 1:], 0.0)
        p5 = jnp.where(lane == 0, f[0][:, :1], 0.0)
        for h in range(HALVES):
            V[t % 2, h, 0] = f[h]
        send_edges(t, p4, p5)

    gather(STEPS - 1)
    gather(STEPS - 2)
    first_edges()

    def advance(s, carry):
        t = STEPS - 1 - s

        @pl.when(t >= 2)
        def _():
            gather(t - 2)

        f = forcing(t - 1)
        ps = [jnp.zeros((ROWS, LANES), F32), jnp.zeros((ROWS, LANES), F32)]

        def put(l, made):
            if l == 0:
                made = [made[h] + f[h] for h in range(HALVES)]
            for h in range(HALVES):
                V[(t - 1) % 2, h, l] = made[h]
            ps[0] = jnp.where(lane == l, made[1][:, LANES - 1:], ps[0])
            ps[1] = jnp.where(lane == l, made[0][:, :1], ps[1])

        stencil(t, put)
        send_edges(t - 1, ps[0], ps[1])
        return carry

    lax.fori_loop(0, STEPS - 1, advance, 0)

    def last(l, made):
        for h in range(HALVES):
            out[l, :, h * LANES:(h + 1) * LANES] = made[h] + BG[h, l]

    stencil(0, last)

    for c in state_copies():
        c.wait_send()

    def drained(buf, sem):
        pltpu.make_async_remote_copy(
            src_ref=buf, dst_ref=buf, send_sem=sem, recv_sem=sem,
            device_id=(down, z), device_id_type=MESH,
        ).wait_send()

    drained(sendA, a_send)
    drained(sendB, b_send)
    drained(HS, h_send)


def shards(sv, bg, res, wgt, ker, cell, cnt):
    def by_step(x):
        return jnp.transpose(x[0], (1, 0, 2)).reshape(STEPS * LANES, LANES)

    anyspace = pl.BlockSpec(memory_space=pl.ANY)
    vmem = pl.BlockSpec(memory_space=pltpu.VMEM)
    dma = pltpu.SemaphoreType.DMA
    return pl.pallas_call(
        kernel,
        out_shape=jax.ShapeDtypeStruct(bg.shape, F32),
        in_specs=[anyspace] * 6 + [vmem],
        out_specs=vmem,
        scratch_shapes=[
            pltpu.VMEM((STEPS + 1, HALVES, NZ, ROWS, LANES), F32),
            pltpu.VMEM((STEPS * LANES, LANES), F32),
            pltpu.VMEM((STEPS * LANES, LANES), F32),
            pltpu.VMEM((STEPS * LANES, LANES), jnp.int32),
            pltpu.VMEM((STEPS * LANES * FOOT, LANES), F32),
            pltpu.VMEM((LANES, LANES), F32),
            pltpu.VMEM((STEPS, NA - 1, FOOT + 1, NI, LANES), F32),
            pltpu.VMEM((STEPS, NA, FOOT + 1, NI, LANES), F32),
            pltpu.VMEM((STEPS, NI - 1, FOOT, 8, LANES), F32),
            pltpu.VMEM((STEPS, NI, FOOT, 8, LANES), F32),
            pltpu.VMEM((STEPS + 1, 6, NZ, LANES), F32),
            pltpu.VMEM((STEPS + 1, 6, NZ, LANES), F32),
            pltpu.VMEM((STEPS, 6, NZ, LANES), F32),
            pltpu.VMEM((STEPS, 6, NZ, LANES), F32),
            pltpu.VMEM((STEPS, 7, HALVES, NZ, ROWS, LANES), F32),
            pltpu.VMEM((HALVES, NZ, ROWS, LANES), F32),
            pltpu.VMEM((HALVES, NZ, ROWS, LANES), F32),
            pltpu.VMEM((2, HALVES, NZ, ROWS, LANES), F32),
            pltpu.VMEM((512, 512), BF16),
            pltpu.VMEM((NA, 2 * FOOT + 2, NI, LANES), F32),
            dma((4,)), dma((4,)), dma, dma((STEPS,)), dma, dma((STEPS,)),
            dma((4,)), dma((4,)), dma, dma((STEPS,)),
        ],
        compiler_params=pltpu.CompilerParams(
            collective_id=0, has_side_effects=True, vmem_limit_bytes=48 * 1024 * 1024
        ),
        cost_estimate=pl.CostEstimate(
            flops=2_000_000_000, bytes_accessed=8_000_000, transcendentals=0
        ),
    )(
        sv, bg, by_step(res), by_step(wgt), by_step(cell),
        ker.reshape(STEPS * LANES * FOOT, LANES), jnp.transpose(cnt[0], (1, 0)),
    )


def solution(mesh):
    in_specs = (
        P(None, None, "lat", "swath"),
        P(None, "lat", "swath"),
        P(("lat", "swath"), None, None, None),
        P(("lat", "swath"), None, None, None),
        P(("lat", "swath"), None, None, None, None),
        P(("lat", "swath"), None, None, None),
        P(("lat", "swath"), None, None),
    )
    return jax.shard_map(
        shards, mesh=mesh, in_specs=in_specs, out_specs=P(None, "lat", "swath"), check_vma=False
    )
```

```python
import functools

import jax
import jax.numpy as jnp
from jax import lax
from jax.experimental import pallas as pl
from jax.experimental.pallas import tpu as pltpu
from jax.sharding import PartitionSpec as P

MESH = pl.DeviceIdType.MESH
F32 = jnp.float32
BF16 = jnp.bfloat16

SAT = 0.45
STEPS = 6
NZ = 16
ROWS = 16
LANES = 128
HALVES = 2
FOOT = 4
WIDE = 3
TALL = 32

NY4 = 4
NI = 8
NZ4 = 4
NA = NY4 * NZ4


def iota(shape, dim):
    return lax.broadcasted_iota(jnp.int32, shape, dim)


def kernel(
    sv, bg, res, wgt, cell, ker, cnt, out,
    X, R, W, C, KV, CT, sendA, recvA, sendB, recvB, RS, RR, CS, CR, FS, FR,
    CF, KK, BG, V, E, PRE,
    in_sem, st_sem, a_send, a_recv, b_send, b_recv, s_send, s_recv, f_send, f_recv,
):
    lat = lax.axis_index("lat")
    z = lax.axis_index("swath")
    y = lat // NI
    me_i = lat % NI
    nlat = NY4 * NI

    loads = [
        pltpu.make_async_copy(res, R, in_sem.at[0]),
        pltpu.make_async_copy(wgt, W, in_sem.at[1]),
        pltpu.make_async_copy(cell, C, in_sem.at[2]),
        pltpu.make_async_copy(ker, KV, in_sem.at[3]),
    ]
    own = pl.ds(0, ROWS)
    states = []
    for h in range(HALVES):
        cols = pl.ds(h * LANES, LANES)
        states.append(
            pltpu.make_async_copy(
                sv.at[:, :, :, cols], X.at[pl.ds(0, STEPS), h, :, own], st_sem.at[h]
            )
        )
        states.append(
            pltpu.make_async_copy(bg.at[:, :, cols], X.at[STEPS, h, :, own], st_sem.at[2 + h])
        )
    for c in loads:
        c.start()
    for c in states:
        c.start()

    up = (lat + nlat - 1) % nlat
    down = (lat + 1) % nlat
    left = (z + NZ4 - 1) % NZ4
    right = (z + 1) % NZ4
    partners = []
    for r in range(1, NA):
        partners.append((((y + r // NZ4) % NY4) * NI + me_i, (z + r % NZ4) % NZ4))
    for k in range(1, NI):
        partners.append((y * NI + (me_i + k) % NI, z))
    for a in (up, down):
        for b in (left, z, right):
            partners.append((a, b))
    barrier = pltpu.get_barrier_semaphore()
    for to in partners:
        pl.semaphore_signal(barrier, inc=1, device_id=to, device_id_type=MESH)

    lane = iota((ROWS, LANES), 1)
    lane8 = iota((8, LANES), 1)
    laneT = iota((TALL, LANES), 1)
    rowT = iota((TALL, LANES), 0)

    counts = [cnt[t].astype(F32) for t in range(STEPS)]
    counts = jnp.concatenate(counts + [jnp.zeros((LANES - STEPS, LANES), F32)], 0)
    CT[...] = jnp.transpose(counts, (1, 0))

    def build(q, carry):
        rr = iota((LANES, 512), 0)
        cc = iota((LANES, 512), 1)
        hit = ((rr >> 6) == (cc >> 8)) & (((rr & 63) * FOOT + q) == (cc & 255))
        E[pl.ds(pl.multiple_of(q * LANES, LANES), LANES), :] = jnp.where(hit, 1.0, 0.0).astype(BF16)
        return carry

    lax.fori_loop(0, FOOT, build, 0)

    for c in loads:
        c.wait()

    lanef = iota((LANES, LANES), 1).astype(F32)
    for t in range(STEPS - 1, -1, -1):
        rows = pl.ds(t * LANES, LANES)
        R[rows, :] = jnp.where(lanef < CT[:, t:t + 1], R[rows, :] * W[rows, :], 0.0)

    def weigh(t, yp, zp):
        d0 = yp * 32 + zp
        rows = pl.ds(t * LANES + d0, NI, stride=4)
        scaled = R[rows, :]
        parts = [
            scaled * KV[pl.ds(d0 * STEPS * FOOT + t * FOOT + j, NI, stride=4 * STEPS * FOOT), :]
            for j in range(FOOT)
        ]
        return parts + [C[rows, :].astype(F32)]

    def partner(r):
        return (y + r // NZ4) % NY4, (z + r % NZ4) % NZ4

    def fill(t):
        for r in range(1, NA):
            for q, part in enumerate(weigh(t, *partner(r))):
                sendA[t, r - 1, q] = part
        for q, part in enumerate(weigh(t, y, z)):
            recvA[t, NA - 1, q] = part

    def stage_a_send(t):
        for r in range(1, NA):
            ty, tz = partner(r)
            pltpu.make_async_remote_copy(
                src_ref=sendA.at[t, r - 1],
                dst_ref=recvA.at[t, r - 1],
                send_sem=a_send,
                recv_sem=a_recv.at[t],
                device_id=(ty * NI + me_i, tz),
                device_id_type=MESH,
            ).start()

    fill(STEPS - 1)
    pl.semaphore_wait(barrier, len(partners))
    stage_a_send(STEPS - 1)

    for c in states:
        c.wait()

    X2 = X.reshape((STEPS + 1) * WIDE * NZ * TALL, LANES)
    widths = [t + 1 for t in range(STEPS)] + [1]
    slices = [(t, k) for t, w in enumerate(widths) for k in range(w)]
    for n, (t, k) in enumerate(slices):
        for h in range(HALVES):
            base = (t * WIDE + h) * NZ * TALL
            RS[0, n, h] = X2[pl.ds(base + ROWS - widths[t] + k, NZ, stride=TALL), :]
            RS[1, n, h] = X2[pl.ds(base + k, NZ, stride=TALL), :]

    def state_columns(t, carry):
        p = [jnp.zeros((ROWS, LANES), F32), jnp.zeros((ROWS, LANES), F32)]
        for l in range(NZ):
            here = (lane >= 8 * l) & (lane < 8 * l + 8)
            for h in range(HALVES):
                x = X[t, h, l, 0:ROWS, :]
                turn = (8 * l + (8 if h == 1 else 0)) % LANES
                if turn:
                    x = pltpu.roll(x, turn, 1)
                p[h] = jnp.where(here, x, p[h])
        for h in range(HALVES):
            for q in range(2):
                CS[h, q, t] = p[h][8 * q:8 * q + 8]
        return carry

    lax.fori_loop(0, STEPS + 1, state_columns, 0)

    def tile_routes(src, dst):
        every = slice(None)
        return [
            (src(every, 1), dst(0, 2), (down, z)),
            (src(every, 0), dst(2, 2), (up, z)),
            (src(1, every), dst(4, 2), (lat, right)),
            (src(0, every), dst(6, 2), (lat, left)),
            (src(1, 1), dst(8, 1), (down, right)),
            (src(0, 1), dst(9, 1), (down, left)),
            (src(1, 0), dst(10, 1), (up, right)),
            (src(0, 0), dst(11, 1), (up, left)),
        ]

    def state_copies():
        pairs = [(RS.at[0], RR.at[0], (down, z)), (RS.at[1], RR.at[1], (up, z))]
        pairs += tile_routes(
            lambda h, q: CS.at[h] if q == slice(None) else CS.at[h, q],
            lambda n, many: CR.at[pl.ds(n - 4, many)] if many == 2 else CR.at[n - 4],
        )[2:]
        return [
            pltpu.make_async_remote_copy(
                src_ref=src, dst_ref=dst, send_sem=s_send.at[n], recv_sem=s_recv.at[n],
                device_id=to, device_id_type=MESH,
            )
            for n, (src, dst, to) in enumerate(pairs)
        ]

    for c in state_copies():
        c.start()

    def stage_a_step(s, carry):
        t = STEPS - 1 - s
        fill(t)
        stage_a_send(t)
        return carry

    lax.fori_loop(1, STEPS, stage_a_step, 0)

    has_up = (lat > 0).astype(F32)
    has_down = (lat < nlat - 1).astype(F32)
    has_left = (z > 0).astype(F32)
    has_right = (z < NZ4 - 1).astype(F32)
    inside = jnp.where(rowT < ROWS, 1.0, jnp.where(rowT < ROWS + 8, has_down, has_up))
    sides = jnp.where(laneT < 64, has_right, has_left)
    masks = [inside, inside, inside * sides]

    def clear(t, carry):
        for g in range(HALVES):
            for l in range(NZ):
                X[t, g, l, ROWS:TALL, :] = jnp.zeros((TALL - ROWS, LANES), F32)
        return carry

    lax.fori_loop(0, STEPS + 1, clear, 0)

    for c in state_copies():
        c.wait_recv()

    for n, (t, k) in enumerate(slices):
        for h in range(HALVES):
            base = (t * WIDE + h) * NZ * TALL
            X2[pl.ds(base + TALL - widths[t] + k, NZ, stride=TALL), :] = RR[0, n, h] * has_up
            X2[pl.ds(base + ROWS + k, NZ, stride=TALL), :] = RR[1, n, h] * has_down

    def third(t, carry):
        from_left = jnp.concatenate([CR[0, t], CR[1, t], CR[6, t], CR[4, t]], 0)
        from_right = jnp.concatenate([CR[2, t], CR[3, t], CR[7, t], CR[5, t]], 0)
        from_left = from_left * (inside * has_left)
        from_right = from_right * (inside * has_right)
        for l in range(NZ):
            a = pltpu.roll(from_left, (120 - 8 * l) % LANES, 1) if l != 15 else from_left
            b = pltpu.roll(from_right, (LANES - 8 * l) % LANES, 1) if l else from_right
            X[t, 2, l] = jnp.where(laneT >= 120, a, jnp.where(laneT < 8, b, 0.0))
        return carry

    lax.fori_loop(0, STEPS + 1, third, 0)

    def to_right(xs):
        turned = [pltpu.roll(x, LANES - 1, 1) for x in xs]
        return [jnp.where(laneT == LANES - 1, turned[(g + 1) % WIDE], turned[g]) for g in range(WIDE)]

    def to_left(xs):
        turned = [pltpu.roll(x, 1, 1) for x in xs]
        return [jnp.where(laneT == 0, turned[(g + WIDE - 1) % WIDE], turned[g]) for g in range(WIDE)]

    def coefficients(s, carry):
        t = STEPS - 1 - s
        before = None
        for l in range(NZ):
            ks = []
            for g in range(WIDE):
                rel = X[t, g, l] * (1.0 / SAT)
                square = rel * rel
                CF[t, 3, g, l] = (0.03 * 3.0) * square
                ks.append(square * rel)
            beside = to_right(ks)
            for g in range(WIDE):
                CF[t, 0, g, l] = 0.05 * (ks[g] + beside[g])
                CF[t, 1, g, l] = 0.05 * (ks[g] + pltpu.roll(ks[g], TALL - 1, 0))
                if l > 0:
                    CF[t, 2, g, l - 1] = 0.125 * (before[g] + ks[g])
            before = ks
        return carry

    lax.fori_loop(0, STEPS, coefficients, 0)

    for l in range(NZ):
        xs = [X[STEPS, g, l] for g in range(WIDE)]
        rights = to_right(xs)
        lefts = to_left(xs)
        for h in range(HALVES):
            near = rights[h] + lefts[h] + (pltpu.roll(xs[h], TALL - 1, 0) + pltpu.roll(xs[h], 1, 0))
            BG[h, l] = (0.9 * xs[h] - 0.1 * near)[:ROWS]

    def blank(l, carry):
        for g in range(WIDE):
            V[(STEPS - 1) % 2, g, l] = jnp.zeros((TALL, LANES), F32)
        return carry

    lax.fori_loop(0, NZ, blank, 0)

    n_iota = iota((LANES, LANES), 0).astype(F32).astype(BF16)
    a_iota = iota((8, LANES), 0).astype(F32)

    def gather(t):
        pltpu.make_async_copy(
            recvA.at[t, pl.ds(0, NA - 1)], recvA.at[t, pl.ds(0, NA - 1)], a_recv.at[t]
        ).wait()

        def split(o, carry):
            anchor = recvA[t, o, FOOT]
            r = jnp.floor(anchor * (1.0 / 64.0))
            b = jnp.floor(anchor * (1.0 / 512.0))
            PRE[o, 8] = (anchor - 64.0 * r) + 64.0 * b
            PRE[o, 9] = r - 8.0 * b
            for j in range(FOOT):
                v = recvA[t, o, j]
                hi = v.astype(BF16).astype(F32)
                PRE[o, 2 * j] = hi
                PRE[o, 2 * j + 1] = v - hi
            return carry

        lax.fori_loop(0, NA, split, 0, unroll=True)

        def tile(k, carry):
            i = (me_i + k) % NI
            def spread(o, q, n):
                return jnp.broadcast_to(PRE[o, q, pl.ds(i, 1), :], (n, LANES))

            lhs, rhs = [], []
            for o in range(NA):
                here = a_iota == spread(o, 9, 8)
                cols = [jnp.where(here, spread(o, q, 8), 0.0) for q in range(2 * FOOT)]
                lhs.append(jnp.concatenate(cols, 0).astype(BF16))
                n_of = jnp.broadcast_to(spread(o, 8, 16).astype(BF16)[:1], (LANES, LANES))
                rhs.append(jnp.where(n_iota == n_of, jnp.ones((), BF16), jnp.zeros((), BF16)))
            acc = lax.dot_general(
                jnp.concatenate(lhs, 1),
                jnp.concatenate(rhs, 1),
                (((1,), (1,)), ((), ())),
                preferred_element_type=F32,
            )
            sums = [acc[16 * j:16 * j + 8] + acc[16 * j + 8:16 * j + 16] for j in range(FOOT)]

            @pl.when(k < NI)
            def _():
                for j in range(FOOT):
                    sendB[t, k - 1, j] = sums[j]
                pltpu.make_async_remote_copy(
                    src_ref=sendB.at[t, k - 1],
                    dst_ref=recvB.at[t, k - 1],
                    send_sem=b_send,
                    recv_sem=b_recv.at[t],
                    device_id=(y * NI + i, z),
                    device_id_type=MESH,
                ).start()

            @pl.when(k == NI)
            def _():
                for j in range(FOOT):
                    recvB[t, NI - 1, j] = sums[j]

            return carry

        lax.fori_loop(1, NI + 1, tile, 0)

    def surface_copies(t):
        def dst(n, many):
            return FR.at[t, pl.ds(n, many)] if many == 2 else FR.at[t, n]

        return [
            pltpu.make_async_remote_copy(
                src_ref=src, dst_ref=to_ref, send_sem=f_send, recv_sem=f_recv.at[t],
                device_id=to, device_id_type=MESH,
            )
            for src, to_ref, to in tile_routes(lambda h, q: FS.at[t, h, q], dst)
        ]

    def forcing(t):
        pltpu.make_async_copy(
            recvB.at[t, pl.ds(0, NI - 1)], recvB.at[t, pl.ds(0, NI - 1)], b_recv.at[t]
        ).wait()
        xs = []
        for j in range(FOOT):
            x = recvB[t, 0, j]
            for k in range(1, NI):
                x = x + recvB[t, k, j]
            xs.append(x)
        x = jnp.concatenate(xs, 1)
        hi = x.astype(BF16).astype(F32)
        both = jnp.concatenate([hi, x - hi], 0).astype(BF16)
        f = jnp.dot(both, E[...], preferred_element_type=F32)
        f = f[:8] + f[8:]
        for h in range(HALVES):
            for q in range(2):
                FS[t, h, q] = f[:, q * 256 + h * LANES:q * 256 + (h + 1) * LANES]
        for c in surface_copies(t):
            c.start()

    def add_surface(t):
        pltpu.make_async_copy(FR.at[t], FR.at[t], f_recv.at[t]).wait()
        wide = [
            jnp.concatenate([FS[t, h, 0], FS[t, h, 1], FR[t, 2 + h], FR[t, h]], 0)
            for h in range(HALVES)
        ]
        sided = [
            jnp.where(lane8 < 64, FR[t, b], FR[t, a])
            for a, b in ((4, 6), (5, 7), (10, 11), (8, 9))
        ]
        wide.append(jnp.concatenate(sided, 0))
        for g in range(WIDE):
            V[t % 2, g, 0] = V[t % 2, g, 0] + wide[g] * masks[g]

    def stencil(t, put):
        slot = t % 2
        add_surface(t)
        over = None
        vs = [V[slot, g, 0] for g in range(WIDE)]
        for l in range(NZ):
            beneath = [V[slot, g, l + 1] for g in range(WIDE)] if l < NZ - 1 else None
            beside = to_right(vs)
            across = [CF[t, 0, g, l] * (beside[g] - vs[g]) for g in range(WIDE)]
            behind = to_left(across)
            made, under = [], []
            for g in range(WIDE):
                v = vs[g]
                along = CF[t, 1, g, l] * (pltpu.roll(v, TALL - 1, 0) - v)
                total = v + (across[g] - behind[g]) + (along - pltpu.roll(along, 1, 0))
                if l < NZ - 1:
                    drop = beneath[g] - v
                    flux = CF[t, 2, g, l] * drop
                    total = total + (flux + CF[t, 3, g, l] * drop)
                    under.append(flux)
                else:
                    total = total - CF[t, 3, g, l] * v
                if l > 0:
                    total = total - over[g]
                made.append(total)
            put(l, made)
            over = under
            vs = beneath

    def step_to_next(t):
        def put(l, made):
            for g in range(WIDE):
                V[(t - 1) % 2, g, l] = made[g] * masks[g]

        stencil(t, put)

    gather(STEPS - 1)
    gather(STEPS - 2)
    forcing(STEPS - 1)

    def advance(s, carry):
        t = STEPS - 1 - s
        gather(t - 2)
        forcing(t - 1)
        step_to_next(t)
        return carry

    lax.fori_loop(0, STEPS - 2, advance, 0)
    forcing(0)
    step_to_next(1)

    def last(l, made):
        for h in range(HALVES):
            out[l, :, h * LANES:(h + 1) * LANES] = made[h][:ROWS] + BG[h, l]

    stencil(0, last)

    for c in state_copies():
        c.wait_send()

    def drained(buf, sem):
        pltpu.make_async_remote_copy(
            src_ref=buf, dst_ref=buf, send_sem=sem, recv_sem=sem,
            device_id=(down, z), device_id_type=MESH,
        ).wait_send()

    drained(sendA, a_send)
    drained(sendB, b_send)
    for t in range(STEPS):
        for c in surface_copies(t):
            c.wait_send()


def shards(sv, bg, res, wgt, ker, cell, cnt):
    def by_step(x):
        return jnp.transpose(x[0], (1, 0, 2)).reshape(STEPS * LANES, LANES)

    anyspace = pl.BlockSpec(memory_space=pltpu.HBM)
    vmem = pl.BlockSpec(memory_space=pltpu.VMEM)
    dma = pltpu.SemaphoreType.DMA
    return pl.pallas_call(
        kernel,
        out_shape=jax.ShapeDtypeStruct(bg.shape, F32),
        in_specs=[anyspace] * 6 + [vmem],
        out_specs=vmem,
        scratch_shapes=[
            pltpu.VMEM((STEPS + 1, WIDE, NZ, TALL, LANES), F32),
            pltpu.VMEM((STEPS * LANES, LANES), F32),
            pltpu.VMEM((STEPS * LANES, LANES), F32),
            pltpu.VMEM((STEPS * LANES, LANES), jnp.int32),
            pltpu.VMEM((STEPS * LANES * FOOT, LANES), F32),
            pltpu.VMEM((LANES, LANES), F32),
            pltpu.VMEM((STEPS, NA - 1, FOOT + 1, NI, LANES), F32),
            pltpu.VMEM((STEPS, NA, FOOT + 1, NI, LANES), F32),
            pltpu.VMEM((STEPS, NI - 1, FOOT, 8, LANES), F32),
            pltpu.VMEM((STEPS, NI, FOOT, 8, LANES), F32),
            pltpu.VMEM((2, 22, HALVES, NZ, LANES), F32),
            pltpu.VMEM((2, 22, HALVES, NZ, LANES), F32),
            pltpu.VMEM((HALVES, 2, STEPS + 1, 8, LANES), F32),
            pltpu.VMEM((8, STEPS + 1, 8, LANES), F32),
            pltpu.VMEM((STEPS, HALVES, 2, 8, LANES), F32),
            pltpu.VMEM((STEPS, 12, 8, LANES), F32),
            pltpu.VMEM((STEPS, 4, WIDE, NZ, TALL, LANES), F32),
            pltpu.VMEM((8, LANES), F32),
            pltpu.VMEM((HALVES, NZ, ROWS, LANES), F32),
            pltpu.VMEM((2, WIDE, NZ, TALL, LANES), F32),
            pltpu.VMEM((512, 512), BF16),
            pltpu.VMEM((NA, 2 * FOOT + 2, NI, LANES), F32),
            dma((4,)), dma((4,)), dma, dma((STEPS,)), dma, dma((STEPS,)),
            dma((8,)), dma((8,)), dma, dma((STEPS,)),
        ],
        compiler_params=pltpu.CompilerParams(
            collective_id=0, has_side_effects=True, vmem_limit_bytes=65200 * 1024
        ),
        cost_estimate=pl.CostEstimate(
            flops=2_000_000_000, bytes_accessed=8_000_000, transcendentals=0
        ),
    )(
        sv, bg, by_step(res), by_step(wgt), by_step(cell),
        ker.reshape(STEPS * LANES * FOOT, LANES), jnp.transpose(cnt, (2, 0, 1)),
    )


def solution(mesh):
    in_specs = (
        P(None, None, "lat", "swath"),
        P(None, "lat", "swath"),
        P(("lat", "swath"), None, None, None),
        P(("lat", "swath"), None, None, None),
        P(("lat", "swath"), None, None, None, None),
        P(("lat", "swath"), None, None, None),
        P(("lat", "swath"), None, None),
    )
    return jax.shard_map(
        shards, mesh=mesh, in_specs=in_specs, out_specs=P(None, "lat", "swath"), check_vma=False
    )
```

```python
import functools

import jax
import jax.numpy as jnp
from jax import lax
from jax.experimental import pallas as pl
from jax.experimental.pallas import tpu as pltpu
from jax.sharding import PartitionSpec as P

MESH = pl.DeviceIdType.MESH
F32 = jnp.float32
BF16 = jnp.bfloat16

SAT = 0.45
STEPS = 6
NZ = 16
ROWS = 16
LANES = 128
HALVES = 2
FOOT = 4
WIDE = 3
TALL = 32

NY4 = 4
NI = 8
NZ4 = 4
NA = NY4 * NZ4


def iota(shape, dim):
    return lax.broadcasted_iota(jnp.int32, shape, dim)


def kernel(
    sv, bg, res, wgt, cell, ker, cnt, out,
    X, R, W, C, KV, CT, sendA, recvA, sendB, recvB, RS, RR, CS, CR, FS, FR,
    CF, KK, BG, V, E, PRE,
    in_sem, st_sem, a_send, a_recv, b_send, b_recv, s_send, s_recv, f_send, f_recv,
):
    lat = lax.axis_index("lat")
    z = lax.axis_index("swath")
    y = lat // NI
    me_i = lat % NI
    nlat = NY4 * NI

    loads = [
        pltpu.make_async_copy(res, R, in_sem.at[0]),
        pltpu.make_async_copy(wgt, W, in_sem.at[1]),
        pltpu.make_async_copy(cell, C, in_sem.at[2]),
        pltpu.make_async_copy(ker, KV, in_sem.at[3]),
    ]
    own = pl.ds(0, ROWS)
    states = []
    for h in range(HALVES):
        cols = pl.ds(h * LANES, LANES)
        states.append(
            pltpu.make_async_copy(
                sv.at[:, :, :, cols], X.at[pl.ds(0, STEPS), h, :, own], st_sem.at[h]
            )
        )
        states.append(
            pltpu.make_async_copy(bg.at[:, :, cols], X.at[STEPS, h, :, own], st_sem.at[2 + h])
        )
    for c in loads:
        c.start()
    for c in states:
        c.start()

    up = (lat + nlat - 1) % nlat
    down = (lat + 1) % nlat
    left = (z + NZ4 - 1) % NZ4
    right = (z + 1) % NZ4
    partners = []
    for r in range(1, NA):
        partners.append((((y + r // NZ4) % NY4) * NI + me_i, (z + r % NZ4) % NZ4))
    for k in range(1, NI):
        partners.append((y * NI + (me_i + k) % NI, z))
    for a in (up, down):
        for b in (left, z, right):
            partners.append((a, b))
    barrier = pltpu.get_barrier_semaphore()
    for to in partners:
        pl.semaphore_signal(barrier, inc=1, device_id=to, device_id_type=MESH)

    lane = iota((ROWS, LANES), 1)
    lane8 = iota((8, LANES), 1)
    laneT = iota((TALL, LANES), 1)
    rowT = iota((TALL, LANES), 0)

    counts = [cnt[t].astype(F32) for t in range(STEPS)]
    counts = jnp.concatenate(counts + [jnp.zeros((LANES - STEPS, LANES), F32)], 0)
    CT[...] = jnp.transpose(counts, (1, 0))

    def build(q, carry):
        rr = iota((LANES, 512), 0)
        cc = iota((LANES, 512), 1)
        hit = ((rr >> 6) == (cc >> 8)) & (((rr & 63) * FOOT + q) == (cc & 255))
        E[pl.ds(pl.multiple_of(q * LANES, LANES), LANES), :] = jnp.where(hit, 1.0, 0.0).astype(BF16)
        return carry

    lax.fori_loop(0, FOOT, build, 0)

    for c in loads:
        c.wait()

    lanef = iota((LANES, LANES), 1).astype(F32)
    for t in range(STEPS - 1, -1, -1):
        rows = pl.ds(t * LANES, LANES)
        R[rows, :] = jnp.where(lanef < CT[:, t:t + 1], R[rows, :] * W[rows, :], 0.0)

    def weigh(t, yp, zp):
        d0 = yp * 32 + zp
        rows = pl.ds(t * LANES + d0, NI, stride=4)
        scaled = R[rows, :]
        parts = [
            scaled * KV[pl.ds(d0 * STEPS * FOOT + t * FOOT + j, NI, stride=4 * STEPS * FOOT), :]
            for j in range(FOOT)
        ]
        return parts + [C[rows, :].astype(F32)]

    def partner(r):
        return (y + r // NZ4) % NY4, (z + r % NZ4) % NZ4

    def fill(t):
        for r in range(1, NA):
            for q, part in enumerate(weigh(t, *partner(r))):
                sendA[t, r - 1, q] = part
        for q, part in enumerate(weigh(t, y, z)):
            recvA[t, NA - 1, q] = part

    def stage_a_send(t):
        for r in range(1, NA):
            ty, tz = partner(r)
            pltpu.make_async_remote_copy(
                src_ref=sendA.at[t, r - 1],
                dst_ref=recvA.at[t, r - 1],
                send_sem=a_send,
                recv_sem=a_recv.at[t],
                device_id=(ty * NI + me_i, tz),
                device_id_type=MESH,
            ).start()

    fill(STEPS - 1)
    pl.semaphore_wait(barrier, len(partners))
    stage_a_send(STEPS - 1)

    for c in states:
        c.wait()

    X2 = X.reshape((STEPS + 1) * WIDE * NZ * TALL, LANES)
    widths = [t + 1 for t in range(STEPS)] + [1]
    slices = [(t, k) for t, w in enumerate(widths) for k in range(w)]
    for n, (t, k) in enumerate(slices):
        for h in range(HALVES):
            base = (t * WIDE + h) * NZ * TALL
            RS[0, n, h] = X2[pl.ds(base + ROWS - widths[t] + k, NZ, stride=TALL), :]
            RS[1, n, h] = X2[pl.ds(base + k, NZ, stride=TALL), :]

    def state_columns(t, carry):
        p = [jnp.zeros((ROWS, LANES), F32), jnp.zeros((ROWS, LANES), F32)]
        for l in range(NZ):
            here = (lane >= 8 * l) & (lane < 8 * l + 8)
            for h in range(HALVES):
                x = X[t, h, l, 0:ROWS, :]
                turn = (8 * l + (8 if h == 1 else 0)) % LANES
                if turn:
                    x = pltpu.roll(x, turn, 1)
                p[h] = jnp.where(here, x, p[h])
        for h in range(HALVES):
            for q in range(2):
                CS[h, q, t] = p[h][8 * q:8 * q + 8]
        return carry

    lax.fori_loop(0, STEPS + 1, state_columns, 0)

    def tile_routes(src, dst):
        every = slice(None)
        return [
            (src(every, 1), dst(0, 2), (down, z)),
            (src(every, 0), dst(2, 2), (up, z)),
            (src(1, every), dst(4, 2), (lat, right)),
            (src(0, every), dst(6, 2), (lat, left)),
            (src(1, 1), dst(8, 1), (down, right)),
            (src(0, 1), dst(9, 1), (down, left)),
            (src(1, 0), dst(10, 1), (up, right)),
            (src(0, 0), dst(11, 1), (up, left)),
        ]

    def state_copies():
        pairs = [(RS.at[0], RR.at[0], (down, z)), (RS.at[1], RR.at[1], (up, z))]
        pairs += tile_routes(
            lambda h, q: CS.at[h] if q == slice(None) else CS.at[h, q],
            lambda n, many: CR.at[pl.ds(n - 4, many)] if many == 2 else CR.at[n - 4],
        )[2:]
        return [
            pltpu.make_async_remote_copy(
                src_ref=src, dst_ref=dst, send_sem=s_send.at[n], recv_sem=s_recv.at[n],
                device_id=to, device_id_type=MESH,
            )
            for n, (src, dst, to) in enumerate(pairs)
        ]

    for c in state_copies():
        c.start()

    def stage_a_step(s, carry):
        t = STEPS - 1 - s
        fill(t)
        stage_a_send(t)
        return carry

    lax.fori_loop(1, 2, stage_a_step, 0)
    for t in range(STEPS - 2):
        fill(t)

    has_up = (lat > 0).astype(F32)
    has_down = (lat < nlat - 1).astype(F32)
    has_left = (z > 0).astype(F32)
    has_right = (z < NZ4 - 1).astype(F32)
    inside = jnp.where(rowT < ROWS, 1.0, jnp.where(rowT < ROWS + 8, has_down, has_up))
    sides = jnp.where(laneT < 64, has_right, has_left)
    masks = [inside, inside, inside * sides]

    def clear(t, carry):
        for g in range(HALVES):
            for l in range(NZ):
                X[t, g, l, ROWS:TALL, :] = jnp.zeros((TALL - ROWS, LANES), F32)
        return carry

    lax.fori_loop(0, STEPS + 1, clear, 0)

    for c in state_copies():
        c.wait_recv()

    for n, (t, k) in enumerate(slices):
        for h in range(HALVES):
            base = (t * WIDE + h) * NZ * TALL
            X2[pl.ds(base + TALL - widths[t] + k, NZ, stride=TALL), :] = RR[0, n, h] * has_up
            X2[pl.ds(base + ROWS + k, NZ, stride=TALL), :] = RR[1, n, h] * has_down

    def third(t, carry):
        from_left = jnp.concatenate([CR[0, t], CR[1, t], CR[6, t], CR[4, t]], 0)
        from_right = jnp.concatenate([CR[2, t], CR[3, t], CR[7, t], CR[5, t]], 0)
        from_left = from_left * (inside * has_left)
        from_right = from_right * (inside * has_right)
        for l in range(NZ):
            a = pltpu.roll(from_left, (120 - 8 * l) % LANES, 1) if l != 15 else from_left
            b = pltpu.roll(from_right, (LANES - 8 * l) % LANES, 1) if l else from_right
            X[t, 2, l] = jnp.where(laneT >= 120, a, jnp.where(laneT < 8, b, 0.0))
        return carry

    lax.fori_loop(0, STEPS + 1, third, 0)

    def to_right(xs):
        turned = [pltpu.roll(x, LANES - 1, 1) for x in xs]
        return [jnp.where(laneT == LANES - 1, turned[(g + 1) % WIDE], turned[g]) for g in range(WIDE)]

    def to_left(xs):
        turned = [pltpu.roll(x, 1, 1) for x in xs]
        return [jnp.where(laneT == 0, turned[(g + WIDE - 1) % WIDE], turned[g]) for g in range(WIDE)]

    def coefficients(s, carry):
        t = STEPS - 1 - s
        before = None
        for l in range(NZ):
            ks = []
            for g in range(WIDE):
                rel = X[t, g, l] * (1.0 / SAT)
                square = rel * rel
                CF[t, 3, g, l] = (0.03 * 3.0) * square
                ks.append(square * rel)
            beside = to_right(ks)
            for g in range(WIDE):
                CF[t, 0, g, l] = 0.05 * (ks[g] + beside[g])
                CF[t, 1, g, l] = 0.05 * (ks[g] + pltpu.roll(ks[g], TALL - 1, 0))
                if l > 0:
                    CF[t, 2, g, l - 1] = 0.125 * (before[g] + ks[g])
            before = ks
        return carry

    lax.fori_loop(0, STEPS, coefficients, 0)

    for l in range(NZ):
        xs = [X[STEPS, g, l] for g in range(WIDE)]
        rights = to_right(xs)
        lefts = to_left(xs)
        for h in range(HALVES):
            near = rights[h] + lefts[h] + (pltpu.roll(xs[h], TALL - 1, 0) + pltpu.roll(xs[h], 1, 0))
            BG[h, l] = (0.9 * xs[h] - 0.1 * near)[:ROWS]

    def blank(l, carry):
        for g in range(WIDE):
            V[(STEPS - 1) % 2, g, l] = jnp.zeros((TALL, LANES), F32)
        return carry

    lax.fori_loop(0, NZ, blank, 0)

    n_iota = iota((LANES, LANES), 0).astype(F32).astype(BF16)
    a_iota = iota((8, LANES), 0).astype(F32)

    def gather(t):
        pltpu.make_async_copy(
            recvA.at[t, pl.ds(0, NA - 1)], recvA.at[t, pl.ds(0, NA - 1)], a_recv.at[t]
        ).wait()

        def split(o, carry):
            anchor = recvA[t, o, FOOT]
            r = jnp.floor(anchor * (1.0 / 64.0))
            b = jnp.floor(anchor * (1.0 / 512.0))
            PRE[o, 8] = (anchor - 64.0 * r) + 64.0 * b
            PRE[o, 9] = r - 8.0 * b
            for j in range(FOOT):
                v = recvA[t, o, j]
                hi = v.astype(BF16).astype(F32)
                PRE[o, 2 * j] = hi
                PRE[o, 2 * j + 1] = v - hi
            return carry

        lax.fori_loop(0, NA, split, 0, unroll=True)

        def tile(k, carry):
            i = (me_i + k) % NI
            def spread(o, q, n):
                return jnp.broadcast_to(PRE[o, q, pl.ds(i, 1), :], (n, LANES))

            lhs, rhs = [], []
            for o in range(NA):
                here = a_iota == spread(o, 9, 8)
                cols = [jnp.where(here, spread(o, q, 8), 0.0) for q in range(2 * FOOT)]
                lhs.append(jnp.concatenate(cols, 0).astype(BF16))
                n_of = jnp.broadcast_to(spread(o, 8, 16).astype(BF16)[:1], (LANES, LANES))
                rhs.append(jnp.where(n_iota == n_of, jnp.ones((), BF16), jnp.zeros((), BF16)))
            acc = lax.dot_general(
                jnp.concatenate(lhs, 1),
                jnp.concatenate(rhs, 1),
                (((1,), (1,)), ((), ())),
                preferred_element_type=F32,
            )
            sums = [acc[16 * j:16 * j + 8] + acc[16 * j + 8:16 * j + 16] for j in range(FOOT)]

            @pl.when(k < NI)
            def _():
                for j in range(FOOT):
                    sendB[t, k - 1, j] = sums[j]
                pltpu.make_async_remote_copy(
                    src_ref=sendB.at[t, k - 1],
                    dst_ref=recvB.at[t, k - 1],
                    send_sem=b_send,
                    recv_sem=b_recv.at[t],
                    device_id=(y * NI + i, z),
                    device_id_type=MESH,
                ).start()

            @pl.when(k == NI)
            def _():
                for j in range(FOOT):
                    recvB[t, NI - 1, j] = sums[j]

            return carry

        lax.fori_loop(1, NI + 1, tile, 0)

    def surface_copies(t):
        def dst(n, many):
            return FR.at[t, pl.ds(n, many)] if many == 2 else FR.at[t, n]

        return [
            pltpu.make_async_remote_copy(
                src_ref=src, dst_ref=to_ref, send_sem=f_send, recv_sem=f_recv.at[t],
                device_id=to, device_id_type=MESH,
            )
            for src, to_ref, to in tile_routes(lambda h, q: FS.at[t, h, q], dst)
        ]

    def forcing(t):
        pltpu.make_async_copy(
            recvB.at[t, pl.ds(0, NI - 1)], recvB.at[t, pl.ds(0, NI - 1)], b_recv.at[t]
        ).wait()
        xs = []
        for j in range(FOOT):
            x = recvB[t, 0, j]
            for k in range(1, NI):
                x = x + recvB[t, k, j]
            xs.append(x)
        x = jnp.concatenate(xs, 1)
        hi = x.astype(BF16).astype(F32)
        both = jnp.concatenate([hi, x - hi], 0).astype(BF16)
        f = jnp.dot(both, E[...], preferred_element_type=F32)
        f = f[:8] + f[8:]
        for h in range(HALVES):
            for q in range(2):
                FS[t, h, q] = f[:, q * 256 + h * LANES:q * 256 + (h + 1) * LANES]
        for c in surface_copies(t):
            c.start()

    def add_surface(t):
        pltpu.make_async_copy(FR.at[t], FR.at[t], f_recv.at[t]).wait()
        wide = [
            jnp.concatenate([FS[t, h, 0], FS[t, h, 1], FR[t, 2 + h], FR[t, h]], 0)
            for h in range(HALVES)
        ]
        sided = [
            jnp.where(lane8 < 64, FR[t, b], FR[t, a])
            for a, b in ((4, 6), (5, 7), (10, 11), (8, 9))
        ]
        wide.append(jnp.concatenate(sided, 0))
        for g in range(WIDE):
            V[t % 2, g, 0] = V[t % 2, g, 0] + wide[g] * masks[g]

    def stencil(t, put):
        slot = t % 2
        add_surface(t)
        over = None
        vs = [V[slot, g, 0] for g in range(WIDE)]
        for l in range(NZ):
            beneath = [V[slot, g, l + 1] for g in range(WIDE)] if l < NZ - 1 else None
            beside = to_right(vs)
            across = [CF[t, 0, g, l] * (beside[g] - vs[g]) for g in range(WIDE)]
            behind = to_left(across)
            made, under = [], []
            for g in range(WIDE):
                v = vs[g]
                along = CF[t, 1, g, l] * (pltpu.roll(v, TALL - 1, 0) - v)
                total = v + (across[g] - behind[g]) + (along - pltpu.roll(along, 1, 0))
                if l < NZ - 1:
                    drop = beneath[g] - v
                    flux = CF[t, 2, g, l] * drop
                    total = total + (flux + CF[t, 3, g, l] * drop)
                    under.append(flux)
                else:
                    total = total - CF[t, 3, g, l] * v
                if l > 0:
                    total = total - over[g]
                made.append(total)
            put(l, made)
            over = under
            vs = beneath

    def step_to_next(t):
        def put(l, made):
            for g in range(WIDE):
                V[(t - 1) % 2, g, l] = made[g] * masks[g]

        stencil(t, put)

    def slot(s, carry):

        @pl.when(s < STEPS - 2)
        def _():
            stage_a_send(STEPS - 1 - 2 - s)

        @pl.when(s < STEPS)
        def _():
            gather(STEPS - 1 - s)

        @pl.when((s >= 2) & (s < STEPS + 2))
        def _():
            forcing(STEPS - 1 + 2 - s)

        @pl.when(s >= 4)
        def _():
            step_to_next(STEPS - 1 + 4 - s)

        return carry

    lax.fori_loop(0, STEPS - 1 + 4, slot, 0)

    def last(l, made):
        for h in range(HALVES):
            out[l, :, h * LANES:(h + 1) * LANES] = made[h][:ROWS] + BG[h, l]

    stencil(0, last)

    for c in state_copies():
        c.wait_send()

    def drained(buf, sem):
        pltpu.make_async_remote_copy(
            src_ref=buf, dst_ref=buf, send_sem=sem, recv_sem=sem,
            device_id=(down, z), device_id_type=MESH,
        ).wait_send()

    drained(sendA, a_send)
    drained(sendB, b_send)
    for t in range(STEPS):
        for c in surface_copies(t):
            c.wait_send()


def shards(sv, bg, res, wgt, ker, cell, cnt):
    def by_step(x):
        return jnp.transpose(x[0], (1, 0, 2)).reshape(STEPS * LANES, LANES)

    anyspace = pl.BlockSpec(memory_space=pltpu.HBM)
    vmem = pl.BlockSpec(memory_space=pltpu.VMEM)
    dma = pltpu.SemaphoreType.DMA
    return pl.pallas_call(
        kernel,
        out_shape=jax.ShapeDtypeStruct(bg.shape, F32),
        in_specs=[anyspace] * 6 + [vmem],
        out_specs=vmem,
        scratch_shapes=[
            pltpu.VMEM((STEPS + 1, WIDE, NZ, TALL, LANES), F32),
            pltpu.VMEM((STEPS * LANES, LANES), F32),
            pltpu.VMEM((STEPS * LANES, LANES), F32),
            pltpu.VMEM((STEPS * LANES, LANES), jnp.int32),
            pltpu.VMEM((STEPS * LANES * FOOT, LANES), F32),
            pltpu.VMEM((LANES, LANES), F32),
            pltpu.VMEM((STEPS, NA - 1, FOOT + 1, NI, LANES), F32),
            pltpu.VMEM((STEPS, NA, FOOT + 1, NI, LANES), F32),
            pltpu.VMEM((STEPS, NI - 1, FOOT, 8, LANES), F32),
            pltpu.VMEM((STEPS, NI, FOOT, 8, LANES), F32),
            pltpu.VMEM((2, 22, HALVES, NZ, LANES), F32),
            pltpu.VMEM((2, 22, HALVES, NZ, LANES), F32),
            pltpu.VMEM((HALVES, 2, STEPS + 1, 8, LANES), F32),
            pltpu.VMEM((8, STEPS + 1, 8, LANES), F32),
            pltpu.VMEM((STEPS, HALVES, 2, 8, LANES), F32),
            pltpu.VMEM((STEPS, 12, 8, LANES), F32),
            pltpu.VMEM((STEPS, 4, WIDE, NZ, TALL, LANES), F32),
            pltpu.VMEM((8, LANES), F32),
            pltpu.VMEM((HALVES, NZ, ROWS, LANES), F32),
            pltpu.VMEM((2, WIDE, NZ, TALL, LANES), F32),
            pltpu.VMEM((512, 512), BF16),
            pltpu.VMEM((NA, 2 * FOOT + 2, NI, LANES), F32),
            dma((4,)), dma((4,)), dma, dma((STEPS,)), dma, dma((STEPS,)),
            dma((8,)), dma((8,)), dma, dma((STEPS,)),
        ],
        compiler_params=pltpu.CompilerParams(
            collective_id=0, has_side_effects=True, vmem_limit_bytes=65200 * 1024
        ),
        cost_estimate=pl.CostEstimate(
            flops=2_000_000_000, bytes_accessed=8_000_000, transcendentals=0
        ),
    )(
        sv, bg, by_step(res), by_step(wgt), by_step(cell),
        ker.reshape(STEPS * LANES * FOOT, LANES), jnp.transpose(cnt, (2, 0, 1)),
    )


def solution(mesh):
    in_specs = (
        P(None, None, "lat", "swath"),
        P(None, "lat", "swath"),
        P(("lat", "swath"), None, None, None),
        P(("lat", "swath"), None, None, None),
        P(("lat", "swath"), None, None, None, None),
        P(("lat", "swath"), None, None, None),
        P(("lat", "swath"), None, None),
    )
    return jax.shard_map(
        shards, mesh=mesh, in_specs=in_specs, out_specs=P(None, "lat", "swath"), check_vma=False
    )
```

```python
import functools

import jax
import jax.numpy as jnp
from jax import lax
from jax.experimental import pallas as pl
from jax.experimental.pallas import tpu as pltpu
from jax.sharding import PartitionSpec as P

MESH = pl.DeviceIdType.MESH
F32 = jnp.float32
BF16 = jnp.bfloat16

SAT = 0.45
STEPS = 6
NZ = 16
ROWS = 16
LANES = 128
HALVES = 2
FOOT = 4
WIDE = 3
TALL = 32

NY4 = 4
NI = 8
NZ4 = 4
NA = NY4 * NZ4


def iota(shape, dim):
    return lax.broadcasted_iota(jnp.int32, shape, dim)


def kernel(
    sv, bg, res, wgt, cell, ker, cnt, out,
    X, R, W, C, KV, CT, sendA, recvA, sendB, recvB, RS, RR, CS, CR, FS, FR,
    CF, KK, BG, V, E, PRE,
    in_sem, st_sem, a_send, a_recv, b_send, b_recv, s_send, s_recv, f_send, f_recv,
):
    lat = lax.axis_index("lat")
    z = lax.axis_index("swath")
    y = lat // NI
    me_i = lat % NI
    nlat = NY4 * NI

    loads = [
        pltpu.make_async_copy(res, R, in_sem.at[0]),
        pltpu.make_async_copy(wgt, W, in_sem.at[1]),
        pltpu.make_async_copy(cell, C, in_sem.at[2]),
        pltpu.make_async_copy(ker, KV, in_sem.at[3]),
    ]
    own = pl.ds(0, ROWS)
    states = []
    for h in range(HALVES):
        cols = pl.ds(h * LANES, LANES)
        states.append(
            pltpu.make_async_copy(
                sv.at[:, :, :, cols], X.at[pl.ds(0, STEPS), h, :, own], st_sem.at[h]
            )
        )
        states.append(
            pltpu.make_async_copy(bg.at[:, :, cols], X.at[STEPS, h, :, own], st_sem.at[2 + h])
        )
    for c in loads:
        c.start()
    for c in states:
        c.start()

    up = (lat + nlat - 1) % nlat
    down = (lat + 1) % nlat
    left = (z + NZ4 - 1) % NZ4
    right = (z + 1) % NZ4
    partners = []
    for r in range(1, NA):
        partners.append((((y + r // NZ4) % NY4) * NI + me_i, (z + r % NZ4) % NZ4))
    for k in range(1, NI):
        partners.append((y * NI + (me_i + k) % NI, z))
    for a in (up, down):
        for b in (left, z, right):
            partners.append((a, b))
    barrier = pltpu.get_barrier_semaphore()
    for to in partners:
        pl.semaphore_signal(barrier, inc=1, device_id=to, device_id_type=MESH)

    lane = iota((ROWS, LANES), 1)
    lane8 = iota((8, LANES), 1)
    laneT = iota((TALL, LANES), 1)
    rowT = iota((TALL, LANES), 0)

    counts = [cnt[t].astype(F32) for t in range(STEPS)]
    counts = jnp.concatenate(counts + [jnp.zeros((LANES - STEPS, LANES), F32)], 0)
    CT[...] = jnp.transpose(counts, (1, 0))

    def build(q, carry):
        rr = iota((LANES, 512), 0)
        cc = iota((LANES, 512), 1)
        hit = ((rr >> 6) == (cc >> 8)) & (((rr & 63) * FOOT + q) == (cc & 255))
        E[pl.ds(pl.multiple_of(q * LANES, LANES), LANES), :] = jnp.where(hit, 1.0, 0.0).astype(BF16)
        return carry

    lax.fori_loop(0, FOOT, build, 0)

    for c in loads:
        c.wait()

    lanef = iota((LANES, LANES), 1).astype(F32)
    for t in range(STEPS - 1, -1, -1):
        rows = pl.ds(t * LANES, LANES)
        R[rows, :] = jnp.where(lanef < CT[:, t:t + 1], R[rows, :] * W[rows, :], 0.0)

    def weigh(t, yp, zp):
        d0 = yp * 32 + zp
        rows = pl.ds(t * LANES + d0, NI, stride=4)
        scaled = R[rows, :]
        parts = [
            scaled * KV[pl.ds(d0 * STEPS * FOOT + t * FOOT + j, NI, stride=4 * STEPS * FOOT), :]
            for j in range(FOOT)
        ]
        return parts + [C[rows, :].astype(F32)]

    def partner(r):
        return (y + r // NZ4) % NY4, (z + r % NZ4) % NZ4

    def fill(t):
        for r in range(1, NA):
            for q, part in enumerate(weigh(t, *partner(r))):
                sendA[t, r - 1, q] = part
        for q, part in enumerate(weigh(t, y, z)):
            recvA[t, NA - 1, q] = part

    def stage_a_send(t):
        for r in range(1, NA):
            ty, tz = partner(r)
            pltpu.make_async_remote_copy(
                src_ref=sendA.at[t, r - 1],
                dst_ref=recvA.at[t, r - 1],
                send_sem=a_send,
                recv_sem=a_recv.at[t],
                device_id=(ty * NI + me_i, tz),
                device_id_type=MESH,
            ).start()

    fill(STEPS - 1)

    for c in states:
        c.wait()

    X2 = X.reshape((STEPS + 1) * WIDE * NZ * TALL, LANES)
    widths = [t + 1 for t in range(STEPS)] + [1]
    slices = [(t, k) for t, w in enumerate(widths) for k in range(w)]
    for n, (t, k) in enumerate(slices):
        for h in range(HALVES):
            base = (t * WIDE + h) * NZ * TALL
            RS[0, n, h] = X2[pl.ds(base + ROWS - widths[t] + k, NZ, stride=TALL), :]
            RS[1, n, h] = X2[pl.ds(base + k, NZ, stride=TALL), :]

    def state_columns(t, carry):
        p = [jnp.zeros((ROWS, LANES), F32), jnp.zeros((ROWS, LANES), F32)]
        for l in range(NZ):
            here = (lane >= 8 * l) & (lane < 8 * l + 8)
            for h in range(HALVES):
                x = X[t, h, l, 0:ROWS, :]
                turn = (8 * l + (8 if h == 1 else 0)) % LANES
                if turn:
                    x = pltpu.roll(x, turn, 1)
                p[h] = jnp.where(here, x, p[h])
        for h in range(HALVES):
            for q in range(2):
                CS[h, q, t] = p[h][8 * q:8 * q + 8]
        return carry

    lax.fori_loop(0, STEPS + 1, state_columns, 0)

    def tile_routes(src, dst):
        every = slice(None)
        return [
            (src(every, 1), dst(0, 2), (down, z)),
            (src(every, 0), dst(2, 2), (up, z)),
            (src(1, every), dst(4, 2), (lat, right)),
            (src(0, every), dst(6, 2), (lat, left)),
            (src(1, 1), dst(8, 1), (down, right)),
            (src(0, 1), dst(9, 1), (down, left)),
            (src(1, 0), dst(10, 1), (up, right)),
            (src(0, 0), dst(11, 1), (up, left)),
        ]

    def state_copies():
        pairs = [(RS.at[0], RR.at[0], (down, z)), (RS.at[1], RR.at[1], (up, z))]
        pairs += tile_routes(
            lambda h, q: CS.at[h] if q == slice(None) else CS.at[h, q],
            lambda n, many: CR.at[pl.ds(n - 4, many)] if many == 2 else CR.at[n - 4],
        )[2:]
        return [
            pltpu.make_async_remote_copy(
                src_ref=src, dst_ref=dst, send_sem=s_send.at[n], recv_sem=s_recv.at[n],
                device_id=to, device_id_type=MESH,
            )
            for n, (src, dst, to) in enumerate(pairs)
        ]

    pl.semaphore_wait(barrier, len(partners))
    for c in state_copies():
        c.start()
    stage_a_send(STEPS - 1)

    def stage_a_step(s, carry):
        t = STEPS - 1 - s
        fill(t)
        stage_a_send(t)
        return carry

    lax.fori_loop(1, 3, stage_a_step, 0)
    for t in range(STEPS - 3):
        fill(t)

    has_up = (lat > 0).astype(F32)
    has_down = (lat < nlat - 1).astype(F32)
    has_left = (z > 0).astype(F32)
    has_right = (z < NZ4 - 1).astype(F32)
    inside = jnp.where(rowT < ROWS, 1.0, jnp.where(rowT < ROWS + 8, has_down, has_up))
    sides = jnp.where(laneT < 64, has_right, has_left)
    masks = [inside, inside, inside * sides]

    def clear(t, carry):
        for g in range(HALVES):
            for l in range(NZ):
                X[t, g, l, ROWS:TALL, :] = jnp.zeros((TALL - ROWS, LANES), F32)
        return carry

    lax.fori_loop(0, STEPS + 1, clear, 0)

    for c in state_copies():
        c.wait_recv()

    for n, (t, k) in enumerate(slices):
        for h in range(HALVES):
            base = (t * WIDE + h) * NZ * TALL
            X2[pl.ds(base + TALL - widths[t] + k, NZ, stride=TALL), :] = RR[0, n, h] * has_up
            X2[pl.ds(base + ROWS + k, NZ, stride=TALL), :] = RR[1, n, h] * has_down

    def third(t, carry):
        from_left = jnp.concatenate([CR[0, t], CR[1, t], CR[6, t], CR[4, t]], 0)
        from_right = jnp.concatenate([CR[2, t], CR[3, t], CR[7, t], CR[5, t]], 0)
        from_left = from_left * (inside * has_left)
        from_right = from_right * (inside * has_right)
        for l in range(NZ):
            a = pltpu.roll(from_left, (120 - 8 * l) % LANES, 1) if l != 15 else from_left
            b = pltpu.roll(from_right, (LANES - 8 * l) % LANES, 1) if l else from_right
            X[t, 2, l] = jnp.where(laneT >= 120, a, jnp.where(laneT < 8, b, 0.0))
        return carry

    lax.fori_loop(0, STEPS + 1, third, 0)

    def to_right(xs):
        turned = [pltpu.roll(x, LANES - 1, 1) for x in xs]
        return [jnp.where(laneT == LANES - 1, turned[(g + 1) % WIDE], turned[g]) for g in range(WIDE)]

    def to_left(xs):
        turned = [pltpu.roll(x, 1, 1) for x in xs]
        return [jnp.where(laneT == 0, turned[(g + WIDE - 1) % WIDE], turned[g]) for g in range(WIDE)]

    def coefficients(s, carry):
        t = STEPS - 1 - s
        before = None
        for l in range(NZ):
            ks = []
            for g in range(WIDE):
                rel = X[t, g, l] * (1.0 / SAT)
                square = rel * rel
                CF[t, 3, g, l] = (0.03 * 3.0) * square
                ks.append(square * rel)
            beside = to_right(ks)
            for g in range(WIDE):
                CF[t, 0, g, l] = 0.05 * (ks[g] + beside[g])
                CF[t, 1, g, l] = 0.05 * (ks[g] + pltpu.roll(ks[g], TALL - 1, 0))
                if l > 0:
                    CF[t, 2, g, l - 1] = 0.125 * (before[g] + ks[g])
            before = ks
        return carry

    lax.fori_loop(0, STEPS, coefficients, 0)

    for l in range(NZ):
        xs = [X[STEPS, g, l] for g in range(WIDE)]
        rights = to_right(xs)
        lefts = to_left(xs)
        for h in range(HALVES):
            near = rights[h] + lefts[h] + (pltpu.roll(xs[h], TALL - 1, 0) + pltpu.roll(xs[h], 1, 0))
            BG[h, l] = (0.9 * xs[h] - 0.1 * near)[:ROWS]

    def blank(l, carry):
        for g in range(WIDE):
            V[(STEPS - 1) % 2, g, l] = jnp.zeros((TALL, LANES), F32)
        return carry

    lax.fori_loop(0, NZ, blank, 0)

    n_iota = iota((LANES, LANES), 0).astype(F32).astype(BF16)
    a_iota = iota((8, LANES), 0).astype(F32)

    def gather(t):
        pltpu.make_async_copy(
            recvA.at[t, pl.ds(0, NA - 1)], recvA.at[t, pl.ds(0, NA - 1)], a_recv.at[t]
        ).wait()

        def split(o, carry):
            anchor = recvA[t, o, FOOT]
            r = jnp.floor(anchor * (1.0 / 64.0))
            b = jnp.floor(anchor * (1.0 / 512.0))
            PRE[o, 8] = (anchor - 64.0 * r) + 64.0 * b
            PRE[o, 9] = r - 8.0 * b
            for j in range(FOOT):
                v = recvA[t, o, j]
                hi = v.astype(BF16).astype(F32)
                PRE[o, 2 * j] = hi
                PRE[o, 2 * j + 1] = v - hi
            return carry

        lax.fori_loop(0, NA, split, 0, unroll=True)

        def tile(k, carry):
            i = (me_i + k) % NI
            def spread(o, q, n):
                return jnp.broadcast_to(PRE[o, q, pl.ds(i, 1), :], (n, LANES))

            lhs, rhs = [], []
            for o in range(NA):
                here = a_iota == spread(o, 9, 8)
                cols = [jnp.where(here, spread(o, q, 8), 0.0) for q in range(2 * FOOT)]
                lhs.append(jnp.concatenate(cols, 0).astype(BF16))
                n_of = jnp.broadcast_to(spread(o, 8, 16).astype(BF16)[:1], (LANES, LANES))
                rhs.append(jnp.where(n_iota == n_of, jnp.ones((), BF16), jnp.zeros((), BF16)))
            acc = lax.dot_general(
                jnp.concatenate(lhs, 1),
                jnp.concatenate(rhs, 1),
                (((1,), (1,)), ((), ())),
                preferred_element_type=F32,
            )
            sums = [acc[16 * j:16 * j + 8] + acc[16 * j + 8:16 * j + 16] for j in range(FOOT)]

            @pl.when(k < NI)
            def _():
                for j in range(FOOT):
                    sendB[t, k - 1, j] = sums[j]
                pltpu.make_async_remote_copy(
                    src_ref=sendB.at[t, k - 1],
                    dst_ref=recvB.at[t, k - 1],
                    send_sem=b_send,
                    recv_sem=b_recv.at[t],
                    device_id=(y * NI + i, z),
                    device_id_type=MESH,
                ).start()

            @pl.when(k == NI)
            def _():
                for j in range(FOOT):
                    recvB[t, NI - 1, j] = sums[j]

            return carry

        lax.fori_loop(1, NI + 1, tile, 0)

    def surface_copies(t):
        def dst(n, many):
            return FR.at[t, pl.ds(n, many)] if many == 2 else FR.at[t, n]

        return [
            pltpu.make_async_remote_copy(
                src_ref=src, dst_ref=to_ref, send_sem=f_send, recv_sem=f_recv.at[t],
                device_id=to, device_id_type=MESH,
            )
            for src, to_ref, to in tile_routes(lambda h, q: FS.at[t, h, q], dst)
        ]

    def forcing(t):
        pltpu.make_async_copy(
            recvB.at[t, pl.ds(0, NI - 1)], recvB.at[t, pl.ds(0, NI - 1)], b_recv.at[t]
        ).wait()
        xs = []
        for j in range(FOOT):
            x = recvB[t, 0, j]
            for k in range(1, NI):
                x = x + recvB[t, k, j]
            xs.append(x)
        x = jnp.concatenate(xs, 1)
        hi = x.astype(BF16).astype(F32)
        both = jnp.concatenate([hi, x - hi], 0).astype(BF16)
        f = jnp.dot(both, E[...], preferred_element_type=F32)
        f = f[:8] + f[8:]
        for h in range(HALVES):
            for q in range(2):
                FS[t, h, q] = f[:, q * 256 + h * LANES:q * 256 + (h + 1) * LANES]
        for c in surface_copies(t):
            c.start()

    def add_surface(t):
        pltpu.make_async_copy(FR.at[t], FR.at[t], f_recv.at[t]).wait()
        wide = [
            jnp.concatenate([FS[t, h, 0], FS[t, h, 1], FR[t, 2 + h], FR[t, h]], 0)
            for h in range(HALVES)
        ]
        sided = [
            jnp.where(lane8 < 64, FR[t, b], FR[t, a])
            for a, b in ((4, 6), (5, 7), (10, 11), (8, 9))
        ]
        wide.append(jnp.concatenate(sided, 0))
        for g in range(WIDE):
            V[t % 2, g, 0] = V[t % 2, g, 0] + wide[g] * masks[g]

    def stencil(t, put):
        slot = t % 2
        add_surface(t)
        over = None
        vs = [V[slot, g, 0] for g in range(WIDE)]
        for l in range(NZ):
            beneath = [V[slot, g, l + 1] for g in range(WIDE)] if l < NZ - 1 else None
            beside = to_right(vs)
            across = [CF[t, 0, g, l] * (beside[g] - vs[g]) for g in range(WIDE)]
            behind = to_left(across)
            made, under = [], []
            for g in range(WIDE):
                v = vs[g]
                along = CF[t, 1, g, l] * (pltpu.roll(v, TALL - 1, 0) - v)
                total = v + (across[g] - behind[g]) + (along - pltpu.roll(along, 1, 0))
                if l < NZ - 1:
                    drop = beneath[g] - v
                    flux = CF[t, 2, g, l] * drop
                    total = total + (flux + CF[t, 3, g, l] * drop)
                    under.append(flux)
                else:
                    total = total - CF[t, 3, g, l] * v
                if l > 0:
                    total = total - over[g]
                made.append(total)
            put(l, made)
            over = under
            vs = beneath

    def step_to_next(t):
        def put(l, made):
            for g in range(WIDE):
                V[(t - 1) % 2, g, l] = made[g] * masks[g]

        stencil(t, put)

    def slot(s, carry):

        @pl.when(s < STEPS - 3)
        def _():
            stage_a_send(STEPS - 1 - 3 - s)

        @pl.when(s < STEPS)
        def _():
            gather(STEPS - 1 - s)

        @pl.when((s >= 2) & (s < STEPS + 2))
        def _():
            forcing(STEPS - 1 + 2 - s)

        @pl.when(s >= 5)
        def _():
            step_to_next(STEPS - 1 + 5 - s)

        return carry

    lax.fori_loop(0, STEPS - 1 + 5, slot, 0)

    def last(l, made):
        for h in range(HALVES):
            out[l, :, h * LANES:(h + 1) * LANES] = made[h][:ROWS] + BG[h, l]

    stencil(0, last)

    for c in state_copies():
        c.wait_send()

    def drained(buf, sem):
        pltpu.make_async_remote_copy(
            src_ref=buf, dst_ref=buf, send_sem=sem, recv_sem=sem,
            device_id=(down, z), device_id_type=MESH,
        ).wait_send()

    drained(sendA, a_send)
    drained(sendB, b_send)
    for t in range(STEPS):
        for c in surface_copies(t):
            c.wait_send()


def shards(sv, bg, res, wgt, ker, cell, cnt):
    def by_step(x):
        return jnp.transpose(x[0], (1, 0, 2)).reshape(STEPS * LANES, LANES)

    anyspace = pl.BlockSpec(memory_space=pltpu.HBM)
    vmem = pl.BlockSpec(memory_space=pltpu.VMEM)
    dma = pltpu.SemaphoreType.DMA
    return pl.pallas_call(
        kernel,
        out_shape=jax.ShapeDtypeStruct(bg.shape, F32),
        in_specs=[anyspace] * 6 + [vmem],
        out_specs=vmem,
        scratch_shapes=[
            pltpu.VMEM((STEPS + 1, WIDE, NZ, TALL, LANES), F32),
            pltpu.VMEM((STEPS * LANES, LANES), F32),
            pltpu.VMEM((STEPS * LANES, LANES), F32),
            pltpu.VMEM((STEPS * LANES, LANES), jnp.int32),
            pltpu.VMEM((STEPS * LANES * FOOT, LANES), F32),
            pltpu.VMEM((LANES, LANES), F32),
            pltpu.VMEM((STEPS, NA - 1, FOOT + 1, NI, LANES), F32),
            pltpu.VMEM((STEPS, NA, FOOT + 1, NI, LANES), F32),
            pltpu.VMEM((STEPS, NI - 1, FOOT, 8, LANES), F32),
            pltpu.VMEM((STEPS, NI, FOOT, 8, LANES), F32),
            pltpu.VMEM((2, 22, HALVES, NZ, LANES), F32),
            pltpu.VMEM((2, 22, HALVES, NZ, LANES), F32),
            pltpu.VMEM((HALVES, 2, STEPS + 1, 8, LANES), F32),
            pltpu.VMEM((8, STEPS + 1, 8, LANES), F32),
            pltpu.VMEM((STEPS, HALVES, 2, 8, LANES), F32),
            pltpu.VMEM((STEPS, 12, 8, LANES), F32),
            pltpu.VMEM((STEPS, 4, WIDE, NZ, TALL, LANES), F32),
            pltpu.VMEM((8, LANES), F32),
            pltpu.VMEM((HALVES, NZ, ROWS, LANES), F32),
            pltpu.VMEM((2, WIDE, NZ, TALL, LANES), F32),
            pltpu.VMEM((512, 512), BF16),
            pltpu.VMEM((NA, 2 * FOOT + 2, NI, LANES), F32),
            dma((4,)), dma((4,)), dma, dma((STEPS,)), dma, dma((STEPS,)),
            dma((8,)), dma((8,)), dma, dma((STEPS,)),
        ],
        compiler_params=pltpu.CompilerParams(
            collective_id=0, has_side_effects=True, vmem_limit_bytes=65200 * 1024
        ),
        cost_estimate=pl.CostEstimate(
            flops=2_000_000_000, bytes_accessed=8_000_000, transcendentals=0
        ),
    )(
        sv, bg, by_step(res), by_step(wgt), by_step(cell),
        ker.reshape(STEPS * LANES * FOOT, LANES), jnp.transpose(cnt, (2, 0, 1)),
    )


def solution(mesh):
    in_specs = (
        P(None, None, "lat", "swath"),
        P(None, "lat", "swath"),
        P(("lat", "swath"), None, None, None),
        P(("lat", "swath"), None, None, None),
        P(("lat", "swath"), None, None, None, None),
        P(("lat", "swath"), None, None, None),
        P(("lat", "swath"), None, None),
    )
    return jax.shard_map(
        shards, mesh=mesh, in_specs=in_specs, out_specs=P(None, "lat", "swath"), check_vma=False
    )
```

```python
import functools

import jax
import jax.numpy as jnp
from jax import lax
from jax.experimental import pallas as pl
from jax.experimental.pallas import tpu as pltpu
from jax.sharding import PartitionSpec as P

MESH = pl.DeviceIdType.MESH
F32 = jnp.float32
BF16 = jnp.bfloat16

SAT = 0.45
STEPS = 6
NZ = 16
ROWS = 16
LANES = 128
HALVES = 2
FOOT = 4
WIDE = 3
TALL = 32

NY4 = 4
NI = 8
NZ4 = 4
NA = NY4 * NZ4


def iota(shape, dim):
    return lax.broadcasted_iota(jnp.int32, shape, dim)


def kernel(
    sv, bg, res, wgt, cell, ker, cnt, out,
    X, R, W, C, KV, CT, sendA, recvA, sendB, recvB, RS, RR, CS, CR, FS, FR,
    CF, KK, BG, V, E, PRE,
    in_sem, st_sem, a_send, a_recv, b_send, b_recv, s_send, s_recv, f_send, f_recv,
):
    lat = lax.axis_index("lat")
    z = lax.axis_index("swath")
    y = lat // NI
    me_i = lat % NI
    nlat = NY4 * NI

    loads = [
        pltpu.make_async_copy(res, R, in_sem.at[0]),
        pltpu.make_async_copy(wgt, W, in_sem.at[1]),
        pltpu.make_async_copy(cell, C, in_sem.at[2]),
        pltpu.make_async_copy(ker, KV, in_sem.at[3]),
    ]
    own = pl.ds(0, ROWS)
    states = []
    for h in range(HALVES):
        cols = pl.ds(h * LANES, LANES)
        states.append(
            pltpu.make_async_copy(
                sv.at[:, :, :, cols], X.at[pl.ds(0, STEPS), h, :, own], st_sem.at[h]
            )
        )
        states.append(
            pltpu.make_async_copy(bg.at[:, :, cols], X.at[STEPS, h, :, own], st_sem.at[2 + h])
        )
    for c in loads:
        c.start()
    for c in states:
        c.start()

    up = (lat + nlat - 1) % nlat
    down = (lat + 1) % nlat
    left = (z + NZ4 - 1) % NZ4
    right = (z + 1) % NZ4
    partners = []
    for r in range(1, NA):
        partners.append((((y + r // NZ4) % NY4) * NI + me_i, (z + r % NZ4) % NZ4))
    for k in range(1, NI):
        partners.append((y * NI + (me_i + k) % NI, z))
    for a in (up, down):
        for b in (left, z, right):
            partners.append((a, b))
    barrier = pltpu.get_barrier_semaphore()
    for to in partners:
        pl.semaphore_signal(barrier, inc=1, device_id=to, device_id_type=MESH)

    lane = iota((ROWS, LANES), 1)
    lane8 = iota((8, LANES), 1)
    laneT = iota((TALL, LANES), 1)
    rowT = iota((TALL, LANES), 0)

    counts = [cnt[t].astype(F32) for t in range(STEPS)]
    counts = jnp.concatenate(counts + [jnp.zeros((LANES - STEPS, LANES), F32)], 0)
    CT[...] = jnp.transpose(counts, (1, 0))

    def build(q, carry):
        rr = iota((LANES, 512), 0)
        cc = iota((LANES, 512), 1)
        hit = ((rr >> 6) == (cc >> 8)) & (((rr & 63) * FOOT + q) == (cc & 255))
        E[pl.ds(pl.multiple_of(q * LANES, LANES), LANES), :] = jnp.where(hit, 1.0, 0.0).astype(BF16)
        return carry

    lax.fori_loop(0, FOOT, build, 0)

    for c in loads:
        c.wait()

    lanef = iota((LANES, LANES), 1).astype(F32)
    for t in range(STEPS - 1, -1, -1):
        rows = pl.ds(t * LANES, LANES)
        R[rows, :] = jnp.where(lanef < CT[:, t:t + 1], R[rows, :] * W[rows, :], 0.0)

    def weigh(t, yp, zp):
        d0 = yp * 32 + zp
        rows = pl.ds(t * LANES + d0, NI, stride=4)
        scaled = R[rows, :]
        parts = [
            scaled * KV[pl.ds(d0 * STEPS * FOOT + t * FOOT + j, NI, stride=4 * STEPS * FOOT), :]
            for j in range(FOOT)
        ]
        return parts + [C[rows, :].astype(F32)]

    def partner(r):
        return (y + r // NZ4) % NY4, (z + r % NZ4) % NZ4

    def fill(t):
        for r in range(1, NA):
            for q, part in enumerate(weigh(t, *partner(r))):
                sendA[t, r - 1, q] = part
        for q, part in enumerate(weigh(t, y, z)):
            recvA[t, NA - 1, q] = part

    def stage_a_send(t):
        for r in range(1, NA):
            ty, tz = partner(r)
            pltpu.make_async_remote_copy(
                src_ref=sendA.at[t, r - 1],
                dst_ref=recvA.at[t, r - 1],
                send_sem=a_send,
                recv_sem=a_recv.at[t],
                device_id=(ty * NI + me_i, tz),
                device_id_type=MESH,
            ).start()

    fill(STEPS - 1)

    for c in states:
        c.wait()

    X2 = X.reshape((STEPS + 1) * WIDE * NZ * TALL, LANES)
    widths = [t + 1 for t in range(STEPS)] + [1]
    slices = [(t, k) for t, w in enumerate(widths) for k in range(w)]
    for n, (t, k) in enumerate(slices):
        for h in range(HALVES):
            base = (t * WIDE + h) * NZ * TALL
            RS[0, n, h] = X2[pl.ds(base + ROWS - widths[t] + k, NZ, stride=TALL), :]
            RS[1, n, h] = X2[pl.ds(base + k, NZ, stride=TALL), :]

    def state_columns(t, carry):
        p = [jnp.zeros((ROWS, LANES), F32), jnp.zeros((ROWS, LANES), F32)]
        for l in range(NZ):
            here = (lane >= 8 * l) & (lane < 8 * l + 8)
            for h in range(HALVES):
                x = X[t, h, l, 0:ROWS, :]
                turn = (8 * l + (8 if h == 1 else 0)) % LANES
                if turn:
                    x = pltpu.roll(x, turn, 1)
                p[h] = jnp.where(here, x, p[h])
        for h in range(HALVES):
            for q in range(2):
                CS[h, q, t] = p[h][8 * q:8 * q + 8]
        return carry

    lax.fori_loop(0, STEPS + 1, state_columns, 0)

    def tile_routes(src, dst):
        every = slice(None)
        return [
            (src(every, 1), dst(0, 2), (down, z)),
            (src(every, 0), dst(2, 2), (up, z)),
            (src(1, every), dst(4, 2), (lat, right)),
            (src(0, every), dst(6, 2), (lat, left)),
            (src(1, 1), dst(8, 1), (down, right)),
            (src(0, 1), dst(9, 1), (down, left)),
            (src(1, 0), dst(10, 1), (up, right)),
            (src(0, 0), dst(11, 1), (up, left)),
        ]

    def state_copies():
        pairs = [(RS.at[0], RR.at[0], (down, z)), (RS.at[1], RR.at[1], (up, z))]
        pairs += tile_routes(
            lambda h, q: CS.at[h] if q == slice(None) else CS.at[h, q],
            lambda n, many: CR.at[pl.ds(n - 4, many)] if many == 2 else CR.at[n - 4],
        )[2:]
        return [
            pltpu.make_async_remote_copy(
                src_ref=src, dst_ref=dst, send_sem=s_send.at[n], recv_sem=s_recv.at[n],
                device_id=to, device_id_type=MESH,
            )
            for n, (src, dst, to) in enumerate(pairs)
        ]

    pl.semaphore_wait(barrier, len(partners))
    for c in state_copies():
        c.start()
    stage_a_send(STEPS - 1)

    def stage_a_step(s, carry):
        t = STEPS - 1 - s
        fill(t)
        stage_a_send(t)
        return carry

    lax.fori_loop(1, 3, stage_a_step, 0)
    for t in range(STEPS - 3):
        fill(t)

    has_up = (lat > 0).astype(F32)
    has_down = (lat < nlat - 1).astype(F32)
    has_left = (z > 0).astype(F32)
    has_right = (z < NZ4 - 1).astype(F32)
    inside = jnp.where(rowT < ROWS, 1.0, jnp.where(rowT < ROWS + 8, has_down, has_up))
    sides = jnp.where(laneT < 64, has_right, has_left)
    masks = [inside, inside, inside * sides]

    def clear(t, carry):
        for g in range(HALVES):
            for l in range(NZ):
                X[t, g, l, ROWS:TALL, :] = jnp.zeros((TALL - ROWS, LANES), F32)
        return carry

    lax.fori_loop(0, STEPS + 1, clear, 0)

    for c in state_copies():
        c.wait_recv()

    for n, (t, k) in enumerate(slices):
        for h in range(HALVES):
            base = (t * WIDE + h) * NZ * TALL
            X2[pl.ds(base + TALL - widths[t] + k, NZ, stride=TALL), :] = RR[0, n, h] * has_up
            X2[pl.ds(base + ROWS + k, NZ, stride=TALL), :] = RR[1, n, h] * has_down

    def third(t, carry):
        from_left = jnp.concatenate([CR[0, t], CR[1, t], CR[6, t], CR[4, t]], 0)
        from_right = jnp.concatenate([CR[2, t], CR[3, t], CR[7, t], CR[5, t]], 0)
        from_left = from_left * (inside * has_left)
        from_right = from_right * (inside * has_right)
        for l in range(NZ):
            a = pltpu.roll(from_left, (120 - 8 * l) % LANES, 1) if l != 15 else from_left
            b = pltpu.roll(from_right, (LANES - 8 * l) % LANES, 1) if l else from_right
            X[t, 2, l] = jnp.where(laneT >= 120, a, jnp.where(laneT < 8, b, 0.0))
        return carry

    lax.fori_loop(0, STEPS + 1, third, 0)

    def to_right(xs):
        turned = [pltpu.roll(x, LANES - 1, 1) for x in xs]
        return [jnp.where(laneT == LANES - 1, turned[(g + 1) % WIDE], turned[g]) for g in range(WIDE)]

    def to_left(xs):
        turned = [pltpu.roll(x, 1, 1) for x in xs]
        return [jnp.where(laneT == 0, turned[(g + WIDE - 1) % WIDE], turned[g]) for g in range(WIDE)]

    def coefficients(s, carry):
        t = STEPS - 1 - s
        before = None
        for l in range(NZ):
            ks = []
            for g in range(WIDE):
                rel = X[t, g, l] * (1.0 / SAT)
                square = rel * rel
                CF[t, 3, g, l] = (0.03 * 3.0) * square
                ks.append(square * rel)
            beside = to_right(ks)
            for g in range(WIDE):
                CF[t, 0, g, l] = 0.05 * (ks[g] + beside[g])
                CF[t, 1, g, l] = 0.05 * (ks[g] + pltpu.roll(ks[g], TALL - 1, 0))
                if l > 0:
                    CF[t, 2, g, l - 1] = 0.125 * (before[g] + ks[g])
            before = ks
        return carry

    lax.fori_loop(0, STEPS, coefficients, 0)

    for l in range(NZ):
        xs = [X[STEPS, g, l] for g in range(WIDE)]
        rights = to_right(xs)
        lefts = to_left(xs)
        for h in range(HALVES):
            near = rights[h] + lefts[h] + (pltpu.roll(xs[h], TALL - 1, 0) + pltpu.roll(xs[h], 1, 0))
            BG[h, l] = (0.9 * xs[h] - 0.1 * near)[:ROWS]

    def blank(l, carry):
        for g in range(WIDE):
            V[(STEPS - 1) % 2, g, l] = jnp.zeros((TALL, LANES), F32)
        return carry

    lax.fori_loop(0, NZ, blank, 0)

    n_iota = iota((LANES, LANES), 0).astype(F32).astype(BF16)
    a_iota = iota((8, LANES), 0).astype(F32)

    def gather(t):
        pltpu.make_async_copy(
            recvA.at[t, pl.ds(0, NA - 1)], recvA.at[t, pl.ds(0, NA - 1)], a_recv.at[t]
        ).wait()

        def split(o, carry):
            anchor = recvA[t, o, FOOT]
            r = jnp.floor(anchor * (1.0 / 64.0))
            b = jnp.floor(anchor * (1.0 / 512.0))
            PRE[o, 8] = (anchor - 64.0 * r) + 64.0 * b
            PRE[o, 9] = r - 8.0 * b
            for j in range(FOOT):
                v = recvA[t, o, j]
                hi = v.astype(BF16).astype(F32)
                PRE[o, 2 * j] = hi
                PRE[o, 2 * j + 1] = v - hi
            return carry

        lax.fori_loop(0, NA, split, 0, unroll=True)

        def tile(k, carry):
            i = (me_i + k) % NI
            def spread(o, q, n):
                return jnp.broadcast_to(PRE[o, q, pl.ds(i, 1), :], (n, LANES))

            lhs, rhs = [], []
            for o in range(NA):
                here = a_iota == spread(o, 9, 8)
                cols = [jnp.where(here, spread(o, q, 8), 0.0) for q in range(2 * FOOT)]
                lhs.append(jnp.concatenate(cols, 0).astype(BF16))
                n_of = jnp.broadcast_to(spread(o, 8, 16).astype(BF16)[:1], (LANES, LANES))
                rhs.append(jnp.where(n_iota == n_of, jnp.ones((), BF16), jnp.zeros((), BF16)))
            acc = lax.dot_general(
                jnp.concatenate(lhs, 1),
                jnp.concatenate(rhs, 1),
                (((1,), (1,)), ((), ())),
                preferred_element_type=F32,
            )
            sums = [acc[16 * j:16 * j + 8] + acc[16 * j + 8:16 * j + 16] for j in range(FOOT)]

            @pl.when(k < NI)
            def _():
                for j in range(FOOT):
                    sendB[t, k - 1, j] = sums[j]
                pltpu.make_async_remote_copy(
                    src_ref=sendB.at[t, k - 1],
                    dst_ref=recvB.at[t, k - 1],
                    send_sem=b_send,
                    recv_sem=b_recv.at[t],
                    device_id=(y * NI + i, z),
                    device_id_type=MESH,
                ).start()

            @pl.when(k == NI)
            def _():
                for j in range(FOOT):
                    recvB[t, NI - 1, j] = sums[j]

            return carry

        lax.fori_loop(1, NI + 1, tile, 0)

    def surface_copies(t):
        def dst(n, many):
            return FR.at[t, pl.ds(n, many)] if many == 2 else FR.at[t, n]

        return [
            pltpu.make_async_remote_copy(
                src_ref=src, dst_ref=to_ref, send_sem=f_send, recv_sem=f_recv.at[t],
                device_id=to, device_id_type=MESH,
            )
            for src, to_ref, to in tile_routes(lambda h, q: FS.at[t, h, q], dst)
        ]

    def forcing(t):
        pltpu.make_async_copy(
            recvB.at[t, pl.ds(0, NI - 1)], recvB.at[t, pl.ds(0, NI - 1)], b_recv.at[t]
        ).wait()
        xs = []
        for j in range(FOOT):
            x = recvB[t, 0, j]
            for k in range(1, NI):
                x = x + recvB[t, k, j]
            xs.append(x)
        x = jnp.concatenate(xs, 1)
        hi = x.astype(BF16).astype(F32)
        both = jnp.concatenate([hi, x - hi], 0).astype(BF16)
        f = jnp.dot(both, E[...], preferred_element_type=F32)
        f = f[:8] + f[8:]
        for h in range(HALVES):
            for q in range(2):
                FS[t, h, q] = f[:, q * 256 + h * LANES:q * 256 + (h + 1) * LANES]
        for c in surface_copies(t):
            c.start()

    def add_surface(t):
        pltpu.make_async_copy(FR.at[t], FR.at[t], f_recv.at[t]).wait()
        wide = [
            jnp.concatenate([FS[t, h, 0], FS[t, h, 1], FR[t, 2 + h], FR[t, h]], 0)
            for h in range(HALVES)
        ]
        sided = [
            jnp.where(lane8 < 64, FR[t, b], FR[t, a])
            for a, b in ((4, 6), (5, 7), (10, 11), (8, 9))
        ]
        wide.append(jnp.concatenate(sided, 0))
        for g in range(WIDE):
            V[t % 2, g, 0] = V[t % 2, g, 0] + wide[g] * masks[g]

    def stencil(t, put):
        slot = t % 2
        add_surface(t)
        over = None
        vs = [V[slot, g, 0] for g in range(WIDE)]
        for l in range(NZ):
            beneath = [V[slot, g, l + 1] for g in range(WIDE)] if l < NZ - 1 else None
            beside = to_right(vs)
            across = [CF[t, 0, g, l] * (beside[g] - vs[g]) for g in range(WIDE)]
            behind = to_left(across)
            made, under = [], []
            for g in range(WIDE):
                v = vs[g]
                along = CF[t, 1, g, l] * (pltpu.roll(v, TALL - 1, 0) - v)
                total = v + (across[g] - behind[g]) + (along - pltpu.roll(along, 1, 0))
                if l < NZ - 1:
                    drop = beneath[g] - v
                    flux = CF[t, 2, g, l] * drop
                    total = total + (flux + CF[t, 3, g, l] * drop)
                    under.append(flux)
                else:
                    total = total - CF[t, 3, g, l] * v
                if l > 0:
                    total = total - over[g]
                made.append(total)
            put(l, made)
            over = under
            vs = beneath

    def step_to_next(t):
        def put(l, made):
            for g in range(WIDE):
                V[(t - 1) % 2, g, l] = made[g] * masks[g]

        stencil(t, put)

    def slot(s, carry):

        @pl.when(s < STEPS - 3)
        def _():
            stage_a_send(STEPS - 1 - 3 - s)

        @pl.when(s < STEPS)
        def _():
            gather(STEPS - 1 - s)

        @pl.when((s >= 2) & (s < STEPS + 2))
        def _():
            forcing(STEPS - 1 + 2 - s)

        @pl.when(s >= 5)
        def _():
            step_to_next(STEPS - 1 + 5 - s)

        return carry

    lax.fori_loop(0, STEPS - 1 + 5, slot, 0)

    def last(l, made):
        for h in range(HALVES):
            out[l, :, h * LANES:(h + 1) * LANES] = made[h][:ROWS] + BG[h, l]

    stencil(0, last)

    for c in state_copies():
        c.wait_send()

    def drained(buf, sem):
        pltpu.make_async_remote_copy(
            src_ref=buf, dst_ref=buf, send_sem=sem, recv_sem=sem,
            device_id=(down, z), device_id_type=MESH,
        ).wait_send()

    drained(sendA, a_send)
    drained(sendB, b_send)
    for t in range(STEPS):
        for c in surface_copies(t):
            c.wait_send()


def shards(sv, bg, res, wgt, ker, cell, cnt):
    def by_step(x):
        return jnp.transpose(x[0], (1, 0, 2)).reshape(STEPS * LANES, LANES)

    anyspace = pl.BlockSpec(memory_space=pltpu.HBM)
    vmem = pl.BlockSpec(memory_space=pltpu.VMEM)
    dma = pltpu.SemaphoreType.DMA
    return pl.pallas_call(
        kernel,
        out_shape=jax.ShapeDtypeStruct(bg.shape, F32),
        in_specs=[anyspace] * 6 + [vmem],
        out_specs=vmem,
        scratch_shapes=[
            pltpu.VMEM((STEPS + 1, WIDE, NZ, TALL, LANES), F32),
            pltpu.VMEM((STEPS * LANES, LANES), F32),
            pltpu.VMEM((STEPS * LANES, LANES), F32),
            pltpu.VMEM((STEPS * LANES, LANES), jnp.int32),
            pltpu.VMEM((STEPS * LANES * FOOT, LANES), F32),
            pltpu.VMEM((LANES, LANES), F32),
            pltpu.VMEM((STEPS, NA - 1, FOOT + 1, NI, LANES), F32),
            pltpu.VMEM((STEPS, NA, FOOT + 1, NI, LANES), F32),
            pltpu.VMEM((STEPS, NI - 1, FOOT, 8, LANES), F32),
            pltpu.VMEM((STEPS, NI, FOOT, 8, LANES), F32),
            pltpu.VMEM((2, 22, HALVES, NZ, LANES), F32),
            pltpu.VMEM((2, 22, HALVES, NZ, LANES), F32),
            pltpu.VMEM((HALVES, 2, STEPS + 1, 8, LANES), F32),
            pltpu.VMEM((8, STEPS + 1, 8, LANES), F32),
            pltpu.VMEM((STEPS, HALVES, 2, 8, LANES), F32),
            pltpu.VMEM((STEPS, 12, 8, LANES), F32),
            pltpu.VMEM((STEPS, 4, WIDE, NZ, TALL, LANES), F32),
            pltpu.VMEM((8, LANES), F32),
            pltpu.VMEM((HALVES, NZ, ROWS, LANES), F32),
            pltpu.VMEM((2, WIDE, NZ, TALL, LANES), F32),
            pltpu.VMEM((512, 512), BF16),
            pltpu.VMEM((NA, 2 * FOOT + 2, NI, LANES), F32),
            dma((4,)), dma((4,)), dma, dma((STEPS,)), dma, dma((STEPS,)),
            dma((8,)), dma((8,)), dma, dma((STEPS,)),
        ],
        compiler_params=pltpu.CompilerParams(
            collective_id=0, has_side_effects=True, vmem_limit_bytes=54800 * 1024
        ),
        cost_estimate=pl.CostEstimate(
            flops=2_000_000_000, bytes_accessed=8_000_000, transcendentals=0
        ),
    )(
        sv, bg, by_step(res), by_step(wgt), by_step(cell),
        ker.reshape(STEPS * LANES * FOOT, LANES), jnp.transpose(cnt, (2, 0, 1)),
    )


def solution(mesh):
    in_specs = (
        P(None, None, "lat", "swath"),
        P(None, "lat", "swath"),
        P(("lat", "swath"), None, None, None),
        P(("lat", "swath"), None, None, None),
        P(("lat", "swath"), None, None, None, None),
        P(("lat", "swath"), None, None, None),
        P(("lat", "swath"), None, None),
    )
    return jax.shard_map(
        shards, mesh=mesh, in_specs=in_specs, out_specs=P(None, "lat", "swath"), check_vma=False
    )
```
